32 devices in a mesh: ctx: 4 (over y, x), ch: 8 (over z, core).
Axes of the slice: x: 2, y: 2, z: 4, core: 2. Of those that a mesh axis runs over, the one named last changes fastest.
Arguments:
- queries: bfloat16 [4096, 4096], P('ctx', 'ch'), may hold values from -12 to 12
- key_input: bfloat16 [4096, 4096], P('ctx', 'ch'), may hold values from -6 to 6
- value_input: bfloat16 [4096, 4096], P('ctx', 'ch'), may hold values from -6 to 6
- filters: bfloat16 [4096, 4096], P('ctx', 'ch'), may hold values from -0.3 to 0.3
- skip_gain: float32 [4096], P('ch'), may hold values from -0.3 to 0.3
- out_weight: bfloat16 [4096, 4096], P('ch'), may hold values from -0.125 to 0.125
Outputs:
- layer_out: bfloat16 [4096, 4096], P('ctx', 'ch')
The draws below stay inside these ranges and needn't reach their ends.
All inputs are finite; a program needn't handle non-finite values.
Results may differ from the reference program's by a relative error of at most 0.019.
Values may be sent and summed in bfloat16 or wider, within the bound.
A program may use at most 320 MiB of HBM per device.

```python
import math
import jax
import jax.numpy as jnp
from jax import lax

D = 4096
TOKENS = 4096
N_CH = 8


def draw_filters(key, part):
    key_pick, key_slow, key_fast, key_head, key_tail, key_weight = jax.random.split(key, 6)
    positions = jnp.arange(TOKENS, dtype=jnp.float32)[:, None]
    slow_rate = jnp.exp(jax.random.uniform(key_slow, (D,), jnp.float32, jnp.log(0.1), jnp.log(1.0))) / TOKENS
    fast_rate = jnp.exp(jax.random.uniform(key_fast, (D,), jnp.float32, jnp.log(1.0 / 60.0), jnp.log(1.0 / 30.0)))
    head_weight = jax.random.uniform(key_weight, (D,), jnp.float32, 0.15, 0.35)
    chosen = jax.random.bernoulli(key_pick, 0.5, (D,))
    head_scale = jnp.where(chosen, head_weight * jnp.sqrt(2.0 * fast_rate), 0.0)
    head_env = head_scale[None, :] * jnp.exp(-fast_rate[None, :] * positions)
    tail_env = 0.13 / math.sqrt(TOKENS) * jnp.exp(-slow_rate[None, :] * positions)
    head_noise = jax.random.truncated_normal(key_head, -3.0, 3.0, (TOKENS, D), jnp.float32)
    tail_noise = jax.random.truncated_normal(key_tail, -3.0, 3.0, (TOKENS, D), jnp.float32)
    return (head_env * head_noise + tail_env * tail_noise).astype(jnp.bfloat16)


def strengthened(result, stream_key, source, target, shards_of, factor):
    def block_of(axis_at):
        return (jnp.arange(result.shape[axis_at]) // (result.shape[axis_at] // shards_of)).reshape((-1,) + (1,) * (result.ndim - 1 - axis_at))

    first = jax.random.permutation(stream_key, shards_of)[block_of(target)]
    far = (block_of(target) + shards_of // 2) % shards_of
    return jnp.where((block_of(source) == first) | (block_of(source) == far), factor * result, result)


def block_levels(rng, shape, cuts, least, largest):
    def one(axis_at, parts):
        steps = jax.random.uniform(jax.random.fold_in(jax.random.fold_in(rng, 6), axis_at), (parts,), jnp.float32, least / len(cuts), largest / len(cuts))
        return jnp.repeat(jnp.exp(steps), shape[axis_at] // parts).reshape((-1,) + (1,) * (len(shape) - axis_at - 1))

    gain = one(*cuts[0])
    for cut in cuts[1:]:
        gain = gain * one(*cut)
    return gain


def scatter_about(own_key, extent, deviation, bound, pieces=(), held_as=jnp.bfloat16):
    array = jax.random.normal(own_key, extent, jnp.float32) * deviation
    if len(pieces) > 0:
        array = block_levels(own_key, extent, pieces, -0.22, 0.18) * array
    return jnp.clip(array, min=-bound, max=bound).astype(held_as)


def noise_with(stream_key, dims, scale, reach, pieces, heavy, held_as=jnp.bfloat16):
    entries = scale * jax.random.normal(stream_key, dims, jnp.float32)
    if pieces:
        entries = entries * block_levels(stream_key, dims, pieces, -0.22, 0.18)
    return jnp.clip(strengthened(entries, jax.random.fold_in(stream_key, 3), *heavy), -reach, reach).astype(held_as)


def setup_inputs(seed: int = 0) -> dict:
    streams_of = jax.random.split(jax.random.key(seed), 7)
    return {
        "queries": scatter_about(streams_of[0], (TOKENS, D), 2.0, 12.0, ((0, 4), (1, 8))),
        "key_input": scatter_about(streams_of[1], (TOKENS, D), 1.0, 6.0, ((0, 4), (1, 8))),
        "value_input": scatter_about(streams_of[2], (TOKENS, D), 1.0, 6.0, ((0, 4), (1, 8))),
        "filters": draw_filters(jax.random.fold_in(streams_of[6], 71), 0),
        "skip_gain": jnp.clip(jax.random.uniform(streams_of[4], (D,), jnp.float32, -0.3, 0.3) * block_levels(streams_of[4], (D,), ((0, 8),), -0.4, 0.0), -0.3, 0.3),
        "out_weight": noise_with(streams_of[5], (D, D), D ** -0.5, 0.125, ((0, 8),), (0, 1, 8, 2.0)),
    }


def reference(queries, key_input, value_input, filters, skip_gain, out_weight):
    mixed_in = (key_input.astype(jnp.float32) * value_input.astype(jnp.float32)).astype(jnp.bfloat16)
    width = D // N_CH
    groups = D // width
    length = 2 * TOKENS

    def convolve(pair):
        signal, kernel = pair
        product = jnp.fft.rfft(signal, n=length, axis=0) * jnp.fft.rfft(kernel, n=length, axis=0)
        return jnp.fft.irfft(product, n=length, axis=0)[:TOKENS]

    signals = mixed_in.astype(jnp.float32).reshape(TOKENS, groups, width).transpose(1, 0, 2)
    kernels = filters.astype(jnp.float32).reshape(TOKENS, groups, width).transpose(1, 0, 2)
    conv = lax.map(convolve, (signals, kernels))
    conv = conv.transpose(1, 0, 2).reshape(TOKENS, D)
    gated = (queries.astype(jnp.float32) * (conv + skip_gain[None, :] * mixed_in.astype(jnp.float32))).astype(jnp.bfloat16)
    gated_parts = gated.reshape(TOKENS, groups, width).transpose(1, 0, 2)
    weight_parts = out_weight.reshape(groups, width, D)

    def accumulate(total, pair):
        part_rows, part_weight = pair
        term = jnp.dot(part_rows, part_weight, preferred_element_type=jnp.float32).astype(jnp.bfloat16)
        term = lax.optimization_barrier(term)
        return total + term.astype(jnp.float32), None

    total, unused = lax.scan(accumulate, jnp.zeros((TOKENS, D), jnp.float32), (gated_parts, weight_parts))
    return total.astype(jnp.bfloat16)
```

```python
import functools

import jax
import jax.numpy as jnp
import numpy as np
from jax import lax
from jax.experimental import pallas as pl
from jax.experimental.pallas import tpu as pltpu
from jax.sharding import PartitionSpec as P

BLOCK = 256
SUB = 128
F32 = jnp.float32
BF16 = jnp.bfloat16


def transform_tables(block):
    k = np.arange(block)[:, None]
    n = np.arange(block)[None, :]
    angle = np.pi * (((2 * k + 1) * n) % (4 * block)) / (2 * block)
    forward = np.concatenate([np.cos(angle), -np.sin(angle)], axis=0)
    backward = np.concatenate([np.cos(angle).T, -np.sin(angle).T], axis=1) / block

    def halves(table):
        high = table.astype(BF16)
        low = (table - high.astype(np.float64)).astype(BF16)
        return high, low

    f_high, f_low = halves(forward)
    b_high, b_low = halves(backward)
    return np.stack([f_high, f_low]), np.stack([b_high, b_low])


def dot(left, right):
    return jnp.dot(left, right, preferred_element_type=F32)


MESH = pl.DeviceIdType.MESH


def layer_kernel(n_ctx, n_ch, relay, q_hbm, k_hbm, v_hbm, h_hbm, skip_ref, f_hbm, b_hbm, w_hbm, out_ref,
                 q_ref, k_ref, v_ref, h_ref, f_ref, b_ref, w_own, wx, we,
                 outbox, inbox, spec, zbuf, ybuf, conv_out, conv_in, g_ref, gx,
                 send_a, send_b, send_c, recv_a, recv_b, recv_c, ge, gex, own,
                 load_sem, table_sem, w_sem, w_send, w_recv, we_send, we_recv, we_fwd,
                 in_send, in_recv, back_send, back_recv, g_send, g_recv,
                 a_send, a_recv, b_send, b_recv, c_send, c_recv, ge_send, ge_recv, gex_send, gex_recv):
    me = lax.axis_index("ctx")
    ch = lax.axis_index("ch")
    chip = lax.div(ch, 2)
    core = lax.rem(ch, 2)
    mate = ch + 1 - 2 * core
    n_chip = n_ch // 2
    tokens, block = out_ref.shape
    width = conv_in.shape[2]
    per = tokens // BLOCK
    has_left = chip > 0
    has_right = chip < n_chip - 1
    left = jnp.maximum(ch - 2, core)
    right = jnp.minimum(ch + 2, n_ch - 2 + core)

    def remote(src, dst, sent, arrived, target):
        return pltpu.make_async_remote_copy(
            src_ref=src, dst_ref=dst, send_sem=sent, recv_sem=arrived,
            device_id=target, device_id_type=MESH,
        )

    def rows_of(r, size=BLOCK):
        return pl.ds(pl.multiple_of(r * size, size), size)

    barrier = pltpu.get_barrier_semaphore()

    def greet(target):
        pl.semaphore_signal(barrier, inc=1, device_id=target, device_id_type=MESH)

    greet({"ch": mate})
    for d in range(1, n_ctx):
        greet({"ctx": lax.rem(me + d, n_ctx)})

    @pl.when(has_left)
    def _():
        greet({"ch": left})
        greet({"ch": left + 1 - 2 * core})

    @pl.when(has_right)
    def _():
        greet({"ch": right})
        greet({"ch": right + 1 - 2 * core})

    def load(a, r):
        source, target = ((k_hbm, k_ref), (v_hbm, v_ref), (h_hbm, h_ref))[a]
        at = rows_of(r)
        return pltpu.make_async_copy(source.at[at], target.at[at], load_sem.at[a, r])

    f_load = pltpu.make_async_copy(f_hbm, f_ref, table_sem.at[0])
    b_load = pltpu.make_async_copy(b_hbm, b_ref, table_sem.at[1])
    q_load = pltpu.make_async_copy(q_hbm, q_ref, table_sem.at[2])

    def lanes_of(chip_at, core_at):
        return pl.ds(pl.multiple_of((chip_at * 2 + core_at) * block, block), block)

    def w_load(t):
        return pltpu.make_async_copy(w_hbm.at[:, lanes_of(t, core)], w_own.at[t], w_sem.at[t])

    def w_copy(t):
        return remote(w_hbm.at[:, lanes_of(t, 1 - core)], wx.at[t], w_send.at[t], w_recv.at[t], {"ch": mate})

    for r in range(per):
        for a in range(3):
            load(a, r).start()
    f_load.start()

    def in_copy(i, r):
        at = rows_of(r)
        return remote(outbox.at[i, at], inbox.at[me, at], in_send.at[i, r], in_recv.at[me, r], {"ctx": i})

    def in_arrival(i, r):
        at = rows_of(r)
        return remote(outbox.at[i, at], inbox.at[i, at], in_send.at[i, r], in_recv.at[i, r], {"ctx": i})

    pl.semaphore_wait(
        barrier, n_ctx + 2 * has_left.astype(jnp.int32) + 2 * has_right.astype(jnp.int32)
    )

    def fill(r, carry):
        for a in range(3):
            load(a, r).wait()
        at = rows_of(r)
        for i in range(n_ctx):
            lanes = slice(i * width, (i + 1) * width)
            mixed = k_ref[at, lanes].astype(F32) * v_ref[at, lanes].astype(F32)
            outbox[i, at, :width] = mixed.astype(BF16)
            outbox[i, at, width:] = h_ref[at, lanes]

            @pl.when(me != i)
            def _():
                in_copy(i, r).start()
        return carry

    lax.fori_loop(0, per, fill, 0)

    low = 1 - lax.div(chip, n_chip // 2)
    is_end = jnp.logical_or(chip == 0, chip == n_chip - 1)
    is_mid = jnp.logical_not(is_end)
    far = (n_chip - 1) * low
    end = (n_chip - 1) * (1 - low)
    across = n_chip - 1 - chip
    inner = 2 - low

    def bit_of(core_at):
        return (1 - core_at) * lax.rem(me, 2) + core_at * lax.div(me, 2)

    bit = bit_of(core)
    partner = (1 - core) * (me + 1 - 2 * lax.rem(me, 2)) + core * lax.rem(me + 2, 4)

    def we_copy(slot, core_at):
        column = inner * (1 - slot) + (n_chip - 1 - inner) * slot
        return remote(w_hbm.at[:, lanes_of(column, core_at)], we.at[slot, core],
                      we_send.at[slot, core_at], we_recv.at[slot, core], {"ch": inner * 2 + core_at})

    def we_arrival(slot, half):
        return remote(we.at[slot, half], we.at[slot, half], we_fwd.at[slot], we_recv.at[slot, half],
                      {"ctx": partner})

    if relay:
        for core_at in range(2):
            @pl.when(jnp.logical_and(is_end, bit_of(core_at) == core))
            def _():
                for slot in range(2):
                    we_copy(slot, core_at).start()

    b_load.start()
    q_load.start()
    for t in range(n_chip):
        w_load(t).start()
        w_copy(t).start()

    def ahead(box, source, r):
        data = box[source, rows_of(r), :]
        spec[source * per + r] = dot(f_ref[0], data) + dot(f_ref[1], data)

    f_load.wait()

    def ahead_own(r, carry):
        ahead(outbox, me, r)
        return carry

    lax.fori_loop(0, per, ahead_own, 0)

    def ahead_others(r, carry):
        for d in range(1, n_ctx):
            source = lax.rem(me + d, n_ctx)
            in_arrival(source, r).wait_recv()
            ahead(inbox, source, r)
        return carry

    lax.fori_loop(0, per, ahead_others, 0)
    b_load.wait()

    rows = 8
    sign = 1.0 - 2.0 * (lax.broadcasted_iota(jnp.int32, (rows, width), 0) % 2).astype(F32)
    done = set()

    def products(m):
        mine = [i * per + m for i in range(n_ctx)]
        need = sorted(set(mine) | {j - 1 for j in mine if j > 0})
        fresh = [j for j in need if j not in done]
        done.update(fresh)
        top_block = max(fresh) + 1

        def one(chunk, carry):
            top = pl.multiple_of(chunk * rows, rows)
            re = pl.ds(top, rows)
            im = pl.ds(pl.multiple_of(BLOCK + top, rows), rows)
            x = [(spec[p, re, :width], spec[p, im, :width]) for p in range(top_block)]
            h = [(spec[p, re, width:], spec[p, im, width:]) for p in range(top_block)]
            z = {}
            for j in fresh:
                zr = zi = None
                for p in range(j + 1):
                    xr, xi = x[p]
                    hr, hi = h[j - p]
                    tr = xr * hr - xi * hi
                    ti = xr * hi + xi * hr
                    zr = tr if zr is None else zr + tr
                    zi = ti if zi is None else zi + ti
                z[j] = (zr, zi)
                zbuf[j, re, :] = zr
                zbuf[j, im, :] = zi

            def get(j):
                return z[j] if j in z else (zbuf[j, re, :], zbuf[j, im, :])

            for i, j in enumerate(mine):
                yr, yi = get(j)
                if j > 0:
                    lr, li = get(j - 1)
                    yr = yr - sign * li
                    yi = yi + sign * lr
                ybuf[i, re, :] = yr
                ybuf[i, im, :] = yi
            return carry

        lax.fori_loop(0, BLOCK // rows, one, 0)

    def back_copy(i, m):
        at = rows_of(m)
        return remote(conv_out.at[i, at], conv_in.at[me, at], back_send.at[i, m], back_recv.at[me, m], {"ctx": i})

    def back_arrival(i, m):
        at = rows_of(m)
        return remote(conv_out.at[i, at], conv_in.at[i, at], back_send.at[i, m], back_recv.at[i, m], {"ctx": i})

    def convolve(m):
        products(m)
        at = rows_of(m)
        for i in range(0, n_ctx, 2):
            data = jnp.concatenate([ybuf[i], ybuf[i + 1]], axis=1)
            high = data.astype(BF16)
            low_part = (data - high.astype(F32)).astype(BF16)
            conv = (dot(b_ref[0], high) + (dot(b_ref[0], low_part) + dot(b_ref[1], high))).astype(BF16)
            for o in range(2):
                part = conv[:, o * width:(o + 1) * width]
                conv_out[i + o, at, :] = part

                @pl.when(me == i + o)
                def _():
                    conv_in[i + o, at, :] = part

                @pl.when(me != i + o)
                def _():
                    back_copy(i + o, m).start()

    def g_copy(m):
        at = rows_of(m)
        return remote(g_ref.at[at], gx.at[at], g_send.at[m], g_recv.at[m], {"ch": mate})

    def gate(m):
        at = rows_of(m)
        for i in range(n_ctx):
            @pl.when(me != i)
            def _():
                back_arrival(i, m).wait_recv()

        for i in range(n_ctx):
            lanes = slice(i * width, (i + 1) * width)
            mixed = outbox[i, at, :width].astype(F32)
            total = conv_in[i, at, :].astype(F32) + skip_ref[:, lanes] * mixed
            g_ref[at, lanes] = (q_ref[at, lanes].astype(F32) * total).astype(BF16)
        g_copy(m).start()

    def share(t, at):
        return dot(g_ref[at, :], w_own[t]) + dot(gx[at, :], wx[t])

    def weights_ready():
        for t in range(n_chip):
            w_load(t).wait()
            w_copy(t).wait()

    if relay:
        n_sub = tokens // SUB
        each = BLOCK // SUB
        to_inner = {"ch": inner * 2 + core}
        to_end = {"ch": end * 2 + core}
        to_across = {"ch": across * 2 + core}

        def sub(s):
            return rows_of(s, SUB)

        def a_from_end(s):
            return remote(send_a.at[sub(s)], recv_a.at[sub(s)], a_send.at[s], a_recv.at[s], to_inner)

        def a_from_mid(s):
            return remote(send_a.at[sub(s)], recv_b.at[sub(s)], a_send.at[s], b_recv.at[s], to_across)

        def b_from_mid(s):
            return remote(send_b.at[sub(s)], recv_b.at[sub(s)], b_send.at[s], b_recv.at[s], to_end)

        def a_arrival(s):
            return remote(send_a.at[sub(s)], recv_a.at[sub(s)], a_send.at[s], a_recv.at[s], to_end)

        def b_arrival(s):
            return remote(send_b.at[sub(s)], recv_b.at[sub(s)], b_send.at[s], b_recv.at[s], to_across)

        def c_copy(s):
            return remote(send_c.at[sub(s)], recv_c.at[sub(s)], c_send.at[s], c_recv.at[s], to_across)

        def ge_copy(s):
            return remote(g_ref.at[sub(s)], ge.at[sub(s)], ge_send.at[s], ge_recv.at[s], to_inner)

        def ge_arrival(s):
            return remote(g_ref.at[sub(s)], ge.at[sub(s)], ge_send.at[s], ge_recv.at[s], to_end)

        def gex_copy(s):
            return remote(ge.at[sub(s)], gex.at[sub(s)], gex_send.at[s], gex_recv.at[s], {"ch": mate})

        def end_step(s, carry):
            part = share(far, sub(s))
            send_a[sub(s), :] = part.astype(BF16)

            @pl.when(s >= 2)
            def _():
                a_from_end(s - 2).wait_send()

            a_from_end(s).start()
            return carry

        def end_first(m):
            @pl.when(is_end)
            def _():
                g_copy(m).wait()
                lax.fori_loop(m * each, (m + 1) * each, end_step, 0)

        def b_step(s):
            part = share(end, sub(s))
            b_arrival(s).wait_recv()
            send_b[sub(s), :] = (part + recv_b[sub(s), :].astype(F32)).astype(BF16)
            b_from_mid(s).start()

        def mid_step(s, carry):
            part = share(far, sub(s))
            a_arrival(s).wait_recv()
            send_a[sub(s), :] = (part + recv_a[sub(s), :].astype(F32)).astype(BF16)
            a_from_mid(s).start()

            @pl.when(s >= 1)
            def _():
                b_step(s - 1)
            return carry

        def mid_first(m):
            @pl.when(is_mid)
            def _():
                g_copy(m).wait()
                lax.fori_loop(m * each, (m + 1) * each, mid_step, 0)

        def pass_weights():
            @pl.when(is_mid)
            def _():
                for slot in range(2):
                    we_arrival(slot, bit).wait_recv()
                    we_arrival(slot, bit).start()

        convolve(0)
        convolve(1)
        q_load.wait()
        gate(0)
        weights_ready()
        end_first(0)
        convolve(2)
        gate(1)
        convolve(3)
        end_first(1)
        pass_weights()
        mid_first(0)
        gate(2)
        end_first(2)
        mid_first(1)
        gate(3)
        end_first(3)
        mid_first(2)
        mid_first(3)

        @pl.when(is_end)
        def _():
            def step(s, carry):
                @pl.when(s < 2)
                def _():
                    a_from_end(n_sub - 2 + s).wait_send()

                @pl.when(s >= 2)
                def _():
                    ge_copy(s - 2).wait_send()

                ge_copy(s).start()
                part = share(chip, sub(s))
                b_arrival(s).wait_recv()
                out_ref[sub(s), :] = (part + recv_b[sub(s), :].astype(F32)).astype(BF16)
                return carry

            lax.fori_loop(0, n_sub, step, 0)
            for s in range(n_sub - 2, n_sub):
                ge_copy(s).wait_send()

        @pl.when(is_mid)
        def _():
            b_step(n_sub - 1)
            for slot in range(2):
                we_arrival(slot, 1 - bit).wait_recv()

            def finish(s):
                c_copy(s).wait_recv()
                out_ref[sub(s), :] = (own[sub(s), :] + recv_c[sub(s), :].astype(F32)).astype(BF16)

            def step(s, carry):
                at = sub(s)
                ge_arrival(s).wait_recv()
                gex_copy(s).start()
                part = share(across, at) + dot(ge[at, :], we[1, core])
                gex_copy(s).wait_recv()
                send_c[at, :] = (part + dot(gex[at, :], we[1, 1 - core])).astype(BF16)
                c_copy(s).start()
                own[at, :] = share(chip, at) + dot(ge[at, :], we[0, core]) + dot(gex[at, :], we[0, 1 - core])

                @pl.when(s >= 1)
                def _():
                    finish(s - 1)
                return carry

            lax.fori_loop(0, n_sub, step, 0)
            finish(n_sub - 1)

            def drain(s, carry):
                a_from_mid(s).wait_send()
                b_from_mid(s).wait_send()
                c_copy(s).wait_send()
                gex_copy(s).wait_send()
                return carry

            lax.fori_loop(0, n_sub, drain, 0)
            for slot in range(2):
                we_arrival(slot, bit).wait_send()

        for core_at in range(2):
            @pl.when(jnp.logical_and(is_end, bit_of(core_at) == core))
            def _():
                for slot in range(2):
                    we_copy(slot, core_at).wait_send()
    else:
        def to_right(t, m):
            at = rows_of(m)
            return remote(send_a.at[t, at], recv_a.at[t, at], a_send.at[t, m], a_recv.at[t, m], {"ch": right})

        def to_left(t, m):
            at = rows_of(m)
            return remote(send_a.at[t, at], recv_b.at[t, at], a_send.at[t, m], b_recv.at[t, m], {"ch": left})

        def arrive_left(t, m):
            at = rows_of(m)
            return remote(send_a.at[t, at], recv_a.at[t, at], a_send.at[t, m], a_recv.at[t, m], {"ch": left})

        def arrive_right(t, m):
            at = rows_of(m)
            return remote(send_a.at[t, at], recv_b.at[t, at], a_send.at[t, m], b_recv.at[t, m], {"ch": right})

        def pass_on(t, m, first, arrived, buffer, copy):
            at = rows_of(m)
            part = share(t, at)

            @pl.when(first)
            def _():
                send_a[t, at, :] = part.astype(BF16)

            @pl.when(jnp.logical_not(first))
            def _():
                arrived(t, m).wait_recv()
                send_a[t, at, :] = (part + buffer[t, at, :].astype(F32)).astype(BF16)

            copy(t, m).start()

        def step(m, carry):
            g_copy(m).wait()
            for d in range(n_chip - 1, 0, -1):
                @pl.when(chip + d < n_chip)
                def _():
                    pass_on(chip + d, m, jnp.logical_not(has_left), arrive_left, recv_a, to_right)

                @pl.when(chip - d >= 0)
                def _():
                    pass_on(chip - d, m, jnp.logical_not(has_right), arrive_right, recv_b, to_left)

            own[rows_of(m), :] = share(chip, rows_of(m))
            return carry

        def finish(m, carry):
            at = rows_of(m)

            @pl.when(has_left)
            def _():
                arrive_left(chip, m).wait_recv()
                own[at, :] += recv_a[chip, at, :].astype(F32)

            @pl.when(has_right)
            def _():
                arrive_right(chip, m).wait_recv()
                own[at, :] += recv_b[chip, at, :].astype(F32)

            out_ref[at, :] = own[at, :].astype(BF16)
            for d in range(n_chip - 1, 0, -1):
                @pl.when(chip + d < n_chip)
                def _():
                    to_right(chip + d, m).wait_send()

                @pl.when(chip - d >= 0)
                def _():
                    to_left(chip - d, m).wait_send()
            return carry

        q_load.wait()
        convolve(0)
        for m in range(1, per):
            convolve(m)
            gate(m - 1)
        gate(per - 1)
        weights_ready()
        lax.fori_loop(0, per, step, 0)
        lax.fori_loop(0, per, finish, 0)

    def drain_ctx(r, carry):
        for i in range(n_ctx):
            @pl.when(me != i)
            def _():
                in_copy(i, r).wait_send()
                back_copy(i, r).wait_send()
        return carry

    lax.fori_loop(0, per, drain_ctx, 0)


def per_device(queries, key_input, value_input, filters, skip_gain, out_weight):
    tokens, channels = queries.shape
    n_ctx = lax.axis_size("ctx")
    n_ch = lax.axis_size("ch")
    n_chip = n_ch // 2
    block = out_weight.shape[1] // n_ch
    width = channels // n_ctx
    per = tokens // BLOCK
    nb = n_ctx * per
    relay = n_chip == 4 and n_ctx == 4 and per == 4
    forward, backward = transform_tables(BLOCK)
    vmem = pl.BlockSpec(memory_space=pltpu.VMEM)
    hbm = pl.BlockSpec(memory_space=pl.ANY)
    dma = pltpu.SemaphoreType.DMA
    n_sub = tokens // SUB
    tiny = (16, 128)
    if relay:
        flows = [(tokens, block)] * 6 + [(tokens, channels)] * 2
        flow_sems = [(n_sub,)] * 10
        we_shape = (2, 2, channels, block)
    else:
        wide = (n_chip, tokens, block)
        flows = [wide, tiny, tiny, wide, wide, tiny, tiny, tiny]
        flow_sems = [(n_chip, per)] * 10
        we_shape = (2, 2, 16, 128)
    return pl.pallas_call(
        functools.partial(layer_kernel, n_ctx, n_ch, relay),
        out_shape=jax.ShapeDtypeStruct((tokens, block), BF16),
        in_specs=[hbm] * 4 + [vmem] + [hbm] * 3,
        out_specs=vmem,
        scratch_shapes=[
            pltpu.VMEM((tokens, channels), BF16),
            pltpu.VMEM((tokens, channels), BF16),
            pltpu.VMEM((tokens, channels), BF16),
            pltpu.VMEM((tokens, channels), BF16),
            pltpu.VMEM(forward.shape, BF16),
            pltpu.VMEM(backward.shape, BF16),
            pltpu.VMEM((n_chip, channels, block), BF16),
            pltpu.VMEM((n_chip, channels, block), BF16),
            pltpu.VMEM(we_shape, BF16),
            pltpu.VMEM((n_ctx, tokens, 2 * width), BF16),
            pltpu.VMEM((n_ctx, tokens, 2 * width), BF16),
            pltpu.VMEM((nb, 2 * BLOCK, 2 * width), F32),
            pltpu.VMEM((nb, 2 * BLOCK, width), F32),
            pltpu.VMEM((n_ctx, 2 * BLOCK, width), F32),
            pltpu.VMEM((n_ctx, tokens, width), BF16),
            pltpu.VMEM((n_ctx, tokens, width), BF16),
            pltpu.VMEM((tokens, channels), BF16),
            pltpu.VMEM((tokens, channels), BF16),
        ] + [pltpu.VMEM(shape, BF16) for shape in flows] + [
            pltpu.VMEM((tokens, block), F32),
            dma((3, per)), dma((3,)), dma((n_chip,)), dma((n_chip,)), dma((n_chip,)),
            dma((2, 2)), dma((2, 2)), dma((2,)),
            dma((n_ctx, per)), dma((n_ctx, per)), dma((n_ctx, per)), dma((n_ctx, per)),
            dma((per,)), dma((per,)),
        ] + [dma(shape) for shape in flow_sems],
        compiler_params=pltpu.CompilerParams(
            collective_id=0, has_side_effects=True, vmem_limit_bytes=60 * 1024 * 1024
        ),
        cost_estimate=pl.CostEstimate(
            flops=28 * n_ctx * tokens * BLOCK * width + 2 * tokens * channels * n_ch * block,
            bytes_accessed=12 * tokens * channels + 2 * channels * n_ch * block, transcendentals=0,
        ),
    )(queries, key_input, value_input, filters, skip_gain[None, :],
      jnp.asarray(forward), jnp.asarray(backward), out_weight)


def solution(mesh):
    in_specs = (
        P("ctx", "ch"),
        P("ctx", "ch"),
        P("ctx", "ch"),
        P("ctx", "ch"),
        P("ch"),
        P("ch", None),
    )
    return jax.shard_map(
        per_device, mesh=mesh, in_specs=in_specs, out_specs=P("ctx", "ch"), check_vma=False
    )
```

```python
import functools

import jax
import jax.numpy as jnp
import numpy as np
from jax import lax
from jax.experimental import pallas as pl
from jax.experimental.pallas import tpu as pltpu
from jax.sharding import PartitionSpec as P

BLOCK = 256
PIECE = 128
SUB = 64
WINDOW = 4
B_LAG = 4
VMEM_MIB = 56
F32 = jnp.float32
BF16 = jnp.bfloat16


def transform_tables(block):
    k = np.arange(block)[:, None]
    n = np.arange(block)[None, :]
    angle = np.pi * (((2 * k + 1) * n) % (4 * block)) / (2 * block)
    forward = np.concatenate([np.cos(angle), -np.sin(angle)], axis=0)
    backward = np.concatenate([np.cos(angle).T, -np.sin(angle).T], axis=1) / block

    def halves(table):
        high = table.astype(BF16)
        low = (table - high.astype(np.float64)).astype(BF16)
        return high, low

    f_high, f_low = halves(forward)
    b_high, b_low = halves(backward)
    return np.stack([f_high, f_low]), np.stack([b_high, b_low])


def dot(left, right):
    return jnp.dot(left, right, preferred_element_type=F32)


MESH = pl.DeviceIdType.MESH


def layer_kernel(n_ctx, n_ch, relay, q_hbm, k_hbm, v_hbm, h_hbm, skip_ref, f_hbm, b_hbm, w_hbm, out_ref,
                 q_ref, k_ref, v_ref, h_ref, f_ref, b_ref, w_own, wx, we,
                 outbox, inbox, spec, zbuf, ybuf, yhigh, ylow, conv_out, conv_in, g_ref, gx,
                 send_a, send_b, send_c, recv_a, recv_b, recv_c, ge, gex, own,
                 load_sem, table_sem, w_sem, w_send, w_recv, we_send, we_recv, we_fwd,
                 in_send, in_recv, back_send, back_recv, g_send, g_recv,
                 a_send, a_recv, b_send, b_recv, c_send, c_recv, ge_send, ge_recv, gex_send, gex_recv):
    me = lax.axis_index("ctx")
    ch = lax.axis_index("ch")
    chip = lax.div(ch, 2)
    core = lax.rem(ch, 2)
    mate = ch + 1 - 2 * core
    n_chip = n_ch // 2
    tokens, block = out_ref.shape
    width = conv_in.shape[2]
    per = tokens // BLOCK
    halves = BLOCK // PIECE
    has_left = chip > 0
    has_right = chip < n_chip - 1
    left = jnp.maximum(ch - 2, core)
    right = jnp.minimum(ch + 2, n_ch - 2 + core)

    def remote(src, dst, sent, arrived, target):
        return pltpu.make_async_remote_copy(
            src_ref=src, dst_ref=dst, send_sem=sent, recv_sem=arrived,
            device_id=target, device_id_type=MESH,
        )

    def rows_of(r, size=BLOCK):
        return pl.ds(pl.multiple_of(r * size, size), size)

    barrier = pltpu.get_barrier_semaphore()

    def greet(target):
        pl.semaphore_signal(barrier, inc=1, device_id=target, device_id_type=MESH)

    greet({"ch": mate})
    for d in range(1, n_ctx):
        greet({"ctx": lax.rem(me + d, n_ctx)})

    @pl.when(has_left)
    def _():
        greet({"ch": left})
        greet({"ch": left + 1 - 2 * core})

    @pl.when(has_right)
    def _():
        greet({"ch": right})
        greet({"ch": right + 1 - 2 * core})

    def load(a, r):
        source, target = ((k_hbm, k_ref), (v_hbm, v_ref), (h_hbm, h_ref))[a]
        at = rows_of(r)
        return pltpu.make_async_copy(source.at[at], target.at[at], load_sem.at[a, r])

    f_load = pltpu.make_async_copy(f_hbm, f_ref, table_sem.at[0])
    b_load = pltpu.make_async_copy(b_hbm, b_ref, table_sem.at[1])
    q_load = pltpu.make_async_copy(q_hbm, q_ref, table_sem.at[2])

    def lanes_of(chip_at, core_at):
        return pl.ds(pl.multiple_of((chip_at * 2 + core_at) * block, block), block)

    def w_load(t):
        return pltpu.make_async_copy(w_hbm.at[:, lanes_of(t, core)], w_own.at[t], w_sem.at[t])

    def w_copy(t):
        return remote(w_hbm.at[:, lanes_of(t, 1 - core)], wx.at[t], w_send.at[t], w_recv.at[t], {"ch": mate})

    for r in range(per):
        for a in range(3):
            load(a, r).start()
    f_load.start()

    def in_copy(i, r):
        at = rows_of(r)
        return remote(outbox.at[i, at], inbox.at[me, at], in_send.at[i, r], in_recv.at[me, r], {"ctx": i})

    def in_arrival(i, r):
        at = rows_of(r)
        return remote(outbox.at[i, at], inbox.at[i, at], in_send.at[i, r], in_recv.at[i, r], {"ctx": i})

    pl.semaphore_wait(
        barrier, n_ctx + 2 * has_left.astype(jnp.int32) + 2 * has_right.astype(jnp.int32)
    )

    def fill(r, carry):
        for a in range(3):
            load(a, r).wait()
        at = rows_of(r)
        for i in range(n_ctx):
            lanes = slice(i * width, (i + 1) * width)
            mixed = k_ref[at, lanes].astype(F32) * v_ref[at, lanes].astype(F32)
            outbox[i, at, :width] = mixed.astype(BF16)
            outbox[i, at, width:] = h_ref[at, lanes]

            @pl.when(me != i)
            def _():
                in_copy(i, r).start()
        return carry

    lax.fori_loop(0, per, fill, 0)

    low = 1 - lax.div(chip, n_chip // 2)
    is_end = jnp.logical_or(chip == 0, chip == n_chip - 1)
    is_mid = jnp.logical_not(is_end)
    far = (n_chip - 1) * low
    end = (n_chip - 1) * (1 - low)
    across = n_chip - 1 - chip
    inner = 2 - low

    def bit_of(core_at):
        return (1 - core_at) * lax.rem(me, 2) + core_at * lax.div(me, 2)

    bit = bit_of(core)
    partner = (1 - core) * (me + 1 - 2 * lax.rem(me, 2)) + core * lax.rem(me + 2, 4)

    def we_copy(slot, core_at):
        column = inner * (1 - slot) + (n_chip - 1 - inner) * slot
        return remote(w_hbm.at[:, lanes_of(column, core_at)], we.at[slot, core],
                      we_send.at[slot, core_at], we_recv.at[slot, core], {"ch": inner * 2 + core_at})

    def we_arrival(slot, half):
        return remote(we.at[slot, half], we.at[slot, half], we_fwd.at[slot], we_recv.at[slot, half],
                      {"ctx": partner})

    if relay:
        for core_at in range(2):
            @pl.when(jnp.logical_and(is_end, bit_of(core_at) == core))
            def _():
                for slot in range(2):
                    we_copy(slot, core_at).start()

    b_load.start()
    q_load.start()
    for t in range(n_chip):
        w_load(t).start()
        w_copy(t).start()

    def ahead(box, source, r):
        data = box[source, rows_of(r), :]
        spec[source * per + r] = dot(f_ref[0], data) + dot(f_ref[1], data)

    f_load.wait()

    def ahead_own(r, carry):
        ahead(outbox, me, r)
        return carry

    lax.fori_loop(0, per, ahead_own, 0)

    def ahead_others(r, carry):
        for d in range(1, n_ctx):
            source = lax.rem(me + d, n_ctx)
            in_arrival(source, r).wait_recv()
            ahead(inbox, source, r)
        return carry

    nb = n_ctx * per
    rows = 8
    sign = 1.0 - 2.0 * (lax.broadcasted_iota(jnp.int32, (rows, width), 0) % 2).astype(F32)

    def parts_of(chunk):
        top = pl.multiple_of(chunk * rows, rows)
        return pl.ds(top, rows), pl.ds(pl.multiple_of(BLOCK + top, rows), rows)

    def is_last(p):
        return p % per == per - 1

    def sums(blocks, late, start, re, im):
        pairs = {j: [p for p in range(j + 1) if (is_last(p) or is_last(j - p)) == late] for j in blocks}
        used = {p for j in blocks for p in pairs[j]} | {j - p for j in blocks for p in pairs[j]}
        x = {p: (spec[p, re, :width], spec[p, im, :width]) for p in used}
        h = {p: (spec[p, re, width:], spec[p, im, width:]) for p in used}
        z = {}
        for j in blocks:
            zr, zi = start[j] if j in start else (None, None)
            for p in pairs[j]:
                xr, xi = x[p]
                hr, hi = h[j - p]
                tr = xr * hr - xi * hi
                ti = xr * hi + xi * hr
                zr = tr if zr is None else zr + tr
                zi = ti if zi is None else zi + ti
            z[j] = (zr, zi)
        return z

    def has_early(j):
        return any(not is_last(p) and not is_last(j - p) for p in range(j + 1))

    early = [j for j in range(nb) if has_early(j)]

    def early_sums(chunk, carry):
        re, im = parts_of(chunk)
        for j, (zr, zi) in sums(early, False, {}, re, im).items():
            zbuf[j, re, :] = zr
            zbuf[j, im, :] = zi
        return carry

    lax.fori_loop(0, per - 1, ahead_others, 0)
    lax.fori_loop(0, BLOCK // rows, early_sums, 0)
    ahead_others(per - 1, 0)
    b_load.wait()
    done = set()

    def products(m):
        mine = [i * per + m for i in range(n_ctx)]
        need = sorted(set(mine) | {j - 1 for j in mine if j > 0})
        fresh = [j for j in need if j not in done]
        done.update(fresh)

        def one(chunk, carry):
            re, im = parts_of(chunk)
            start = {j: (zbuf[j, re, :], zbuf[j, im, :]) for j in fresh if j in early}
            z = sums(fresh, True, start, re, im)
            for j in fresh:
                zbuf[j, re, :] = z[j][0]
                zbuf[j, im, :] = z[j][1]

            def get(j):
                return z[j] if j in z else (zbuf[j, re, :], zbuf[j, im, :])

            for i, j in enumerate(mine):
                yr, yi = get(j)
                if j > 0:
                    lr, li = get(j - 1)
                    yr = yr - sign * li
                    yi = yi + sign * lr
                ybuf[i, re, :] = yr
                ybuf[i, im, :] = yi
            return carry

        lax.fori_loop(0, BLOCK // rows, one, 0)
        for i in range(0, n_ctx, 2):
            data = jnp.concatenate([ybuf[i], ybuf[i + 1]], axis=1)
            high = data.astype(BF16)
            yhigh[i // 2] = high
            ylow[i // 2] = (data - high.astype(F32)).astype(BF16)

    def piece(m):
        return rows_of(m, PIECE)

    def back_copy(i, m):
        at = piece(m)
        return remote(conv_out.at[i, at], conv_in.at[me, at], back_send.at[i, m], back_recv.at[me, m], {"ctx": i})

    def back_arrival(i, m):
        at = piece(m)
        return remote(conv_out.at[i, at], conv_in.at[i, at], back_send.at[i, m], back_recv.at[i, m], {"ctx": i})

    def inverse(m):
        at = piece(m)
        inside = slice((m % halves) * PIECE, (m % halves + 1) * PIECE)
        b_high = b_ref[0, inside, :]
        b_low = b_ref[1, inside, :]
        for i in range(0, n_ctx, 2):
            high = yhigh[i // 2]
            conv = (dot(b_high, high) + (dot(b_high, ylow[i // 2]) + dot(b_low, high))).astype(BF16)
            for o in range(2):
                part = conv[:, o * width:(o + 1) * width]
                conv_out[i + o, at, :] = part

                @pl.when(me == i + o)
                def _():
                    conv_in[i + o, at, :] = part

                @pl.when(me != i + o)
                def _():
                    back_copy(i + o, m).start()

    def g_copy(m):
        at = piece(m)
        return remote(g_ref.at[at], gx.at[at], g_send.at[m], g_recv.at[m], {"ch": mate})

    def gate(m):
        at = piece(m)
        for i in range(n_ctx):
            @pl.when(me != i)
            def _():
                back_arrival(i, m).wait_recv()

        for i in range(n_ctx):
            lanes = slice(i * width, (i + 1) * width)
            mixed = outbox[i, at, :width].astype(F32)
            total = conv_in[i, at, :].astype(F32) + skip_ref[:, lanes] * mixed
            g_ref[at, lanes] = (q_ref[at, lanes].astype(F32) * total).astype(BF16)
        g_copy(m).start()

    def share(t, at):
        return dot(g_ref[at, :], w_own[t]) + dot(gx[at, :], wx[t])

    def weights_ready():
        for t in range(n_chip):
            w_load(t).wait()
            w_copy(t).wait()

    if relay:
        n_sub = tokens // SUB
        each = PIECE // SUB
        n_piece = tokens // PIECE
        to_inner = {"ch": inner * 2 + core}
        to_end = {"ch": end * 2 + core}
        to_across = {"ch": across * 2 + core}

        def sub(s):
            return rows_of(s, SUB)

        def a_from_end(s):
            return remote(send_a.at[sub(s)], recv_a.at[sub(s)], a_send.at[s], a_recv.at[s], to_inner)

        def a_from_mid(s):
            return remote(send_a.at[sub(s)], recv_b.at[sub(s)], a_send.at[s], b_recv.at[s], to_across)

        def b_from_mid(s):
            return remote(send_b.at[sub(s)], recv_b.at[sub(s)], b_send.at[s], b_recv.at[s], to_end)

        def a_arrival(s):
            return remote(send_a.at[sub(s)], recv_a.at[sub(s)], a_send.at[s], a_recv.at[s], to_end)

        def b_arrival(s):
            return remote(send_b.at[sub(s)], recv_b.at[sub(s)], b_send.at[s], b_recv.at[s], to_across)

        def c_copy(s):
            return remote(send_c.at[sub(s)], recv_c.at[sub(s)], c_send.at[s], c_recv.at[s], to_across)

        def ge_copy(s):
            return remote(g_ref.at[sub(s)], ge.at[sub(s)], ge_send.at[s], ge_recv.at[s], to_inner)

        def ge_arrival(s):
            return remote(g_ref.at[sub(s)], ge.at[sub(s)], ge_send.at[s], ge_recv.at[s], to_end)

        def gex_copy(s):
            return remote(ge.at[sub(s)], gex.at[sub(s)], gex_send.at[s], gex_recv.at[s], {"ch": mate})

        def end_first(m):
            @pl.when(is_end)
            def _():
                g_copy(m).wait()
                part = share(far, piece(m))
                for o in range(each):
                    s = m * each + o
                    send_a[sub(s), :] = part[o * SUB:(o + 1) * SUB].astype(BF16)
                    if s >= WINDOW:
                        a_from_end(s - WINDOW).wait_send()
                    a_from_end(s).start()

        def b_step(s):
            b_arrival(s).wait_recv()
            send_b[sub(s), :] = (own[sub(s), :] + recv_b[sub(s), :].astype(F32)).astype(BF16)
            b_from_mid(s).start()

        def mid_first(m):
            @pl.when(is_mid)
            def _():
                g_copy(m).wait()
                own[piece(m), :] = share(end, piece(m))
                part = share(far, piece(m))
                for o in range(each):
                    s = m * each + o
                    a_arrival(s).wait_recv()
                    send_a[sub(s), :] = (
                        part[o * SUB:(o + 1) * SUB] + recv_a[sub(s), :].astype(F32)
                    ).astype(BF16)
                    a_from_mid(s).start()
                    if s >= B_LAG:
                        b_step(s - B_LAG)

        def pass_weights():
            @pl.when(is_mid)
            def _():
                for slot in range(2):
                    we_arrival(slot, bit).wait_recv()
                    we_arrival(slot, bit).start()

        products(0)
        inverse(0)
        inverse(1)
        products(1)
        q_load.wait()
        gate(0)
        weights_ready()
        inverse(2)
        end_first(0)
        gate(1)
        inverse(3)
        end_first(1)
        products(2)
        gate(2)
        inverse(4)
        end_first(2)
        mid_first(0)
        gate(3)
        inverse(5)
        end_first(3)
        mid_first(1)
        products(3)
        inverse(6)
        inverse(7)
        pass_weights()
        for m in range(4, 8):
            gate(m)
            end_first(m)
            mid_first(m - 2)
        mid_first(6)
        mid_first(7)

        @pl.when(is_end)
        def _():
            for s in range(n_sub - WINDOW, n_sub):
                a_from_end(s).wait_send()

            def step(p, carry):
                for o in range(each):
                    s = p * each + o

                    @pl.when(s >= WINDOW)
                    def _():
                        ge_copy(s - WINDOW).wait_send()

                    ge_copy(s).start()
                at = piece(p)
                part = share(chip, at)
                for o in range(each):
                    b_arrival(p * each + o).wait_recv()
                out_ref[at, :] = (part + recv_b[at, :].astype(F32)).astype(BF16)
                return carry

            lax.fori_loop(0, n_piece, step, 0)
            for s in range(n_sub - WINDOW, n_sub):
                ge_copy(s).wait_send()

        @pl.when(is_mid)
        def _():
            for s in range(n_sub - B_LAG, n_sub):
                b_step(s)
            for slot in range(2):
                we_arrival(slot, 1 - bit).wait_recv()

            def finish(p):
                at = piece(p)
                for o in range(each):
                    c_copy(p * each + o).wait_recv()
                out_ref[at, :] = (own[at, :] + recv_c[at, :].astype(F32)).astype(BF16)

            def step(p, carry):
                at = piece(p)
                for o in range(each):
                    ge_arrival(p * each + o).wait_recv()
                    gex_copy(p * each + o).start()
                part = share(across, at) + dot(ge[at, :], we[1, core])
                own[at, :] = share(chip, at) + dot(ge[at, :], we[0, core])
                for o in range(each):
                    gex_copy(p * each + o).wait_recv()
                send_c[at, :] = (part + dot(gex[at, :], we[1, 1 - core])).astype(BF16)
                for o in range(each):
                    c_copy(p * each + o).start()
                own[at, :] += dot(gex[at, :], we[0, 1 - core])

                @pl.when(p >= 2)
                def _():
                    finish(p - 2)
                return carry

            lax.fori_loop(0, n_piece, step, 0)
            for p in range(n_piece - 2, n_piece):
                finish(p)

            def drain(s, carry):
                a_from_mid(s).wait_send()
                b_from_mid(s).wait_send()
                c_copy(s).wait_send()
                gex_copy(s).wait_send()
                return carry

            lax.fori_loop(0, n_sub, drain, 0)
            for slot in range(2):
                we_arrival(slot, bit).wait_send()

        for core_at in range(2):
            @pl.when(jnp.logical_and(is_end, bit_of(core_at) == core))
            def _():
                for slot in range(2):
                    we_copy(slot, core_at).wait_send()
    else:
        def to_right(t, m):
            at = rows_of(m)
            return remote(send_a.at[t, at], recv_a.at[t, at], a_send.at[t, m], a_recv.at[t, m], {"ch": right})

        def to_left(t, m):
            at = rows_of(m)
            return remote(send_a.at[t, at], recv_b.at[t, at], a_send.at[t, m], b_recv.at[t, m], {"ch": left})

        def arrive_left(t, m):
            at = rows_of(m)
            return remote(send_a.at[t, at], recv_a.at[t, at], a_send.at[t, m], a_recv.at[t, m], {"ch": left})

        def arrive_right(t, m):
            at = rows_of(m)
            return remote(send_a.at[t, at], recv_b.at[t, at], a_send.at[t, m], b_recv.at[t, m], {"ch": right})

        def pass_on(t, m, first, arrived, buffer, copy):
            at = rows_of(m)
            part = share(t, at)

            @pl.when(first)
            def _():
                send_a[t, at, :] = part.astype(BF16)

            @pl.when(jnp.logical_not(first))
            def _():
                arrived(t, m).wait_recv()
                send_a[t, at, :] = (part + buffer[t, at, :].astype(F32)).astype(BF16)

            copy(t, m).start()

        def step(m, carry):
            for o in range(halves):
                g_copy(m * halves + o).wait()
            for d in range(n_chip - 1, 0, -1):
                @pl.when(chip + d < n_chip)
                def _():
                    pass_on(chip + d, m, jnp.logical_not(has_left), arrive_left, recv_a, to_right)

                @pl.when(chip - d >= 0)
                def _():
                    pass_on(chip - d, m, jnp.logical_not(has_right), arrive_right, recv_b, to_left)

            own[rows_of(m), :] = share(chip, rows_of(m))
            return carry

        def finish(m, carry):
            at = rows_of(m)

            @pl.when(has_left)
            def _():
                arrive_left(chip, m).wait_recv()
                own[at, :] += recv_a[chip, at, :].astype(F32)

            @pl.when(has_right)
            def _():
                arrive_right(chip, m).wait_recv()
                own[at, :] += recv_b[chip, at, :].astype(F32)

            out_ref[at, :] = own[at, :].astype(BF16)
            for d in range(n_chip - 1, 0, -1):
                @pl.when(chip + d < n_chip)
                def _():
                    to_right(chip + d, m).wait_send()

                @pl.when(chip - d >= 0)
                def _():
                    to_left(chip - d, m).wait_send()
            return carry

        q_load.wait()
        for m in range(per):
            products(m)
            for o in range(halves):
                inverse(m * halves + o)
            if m > 0:
                for o in range(halves):
                    gate((m - 1) * halves + o)
        for o in range(halves):
            gate((per - 1) * halves + o)
        weights_ready()
        lax.fori_loop(0, per, step, 0)
        lax.fori_loop(0, per, finish, 0)

    def drain_ctx(r, carry):
        for i in range(n_ctx):
            @pl.when(me != i)
            def _():
                in_copy(i, r).wait_send()
                for o in range(halves):
                    back_copy(i, r * halves + o).wait_send()
        return carry

    lax.fori_loop(0, per, drain_ctx, 0)


def per_device(queries, key_input, value_input, filters, skip_gain, out_weight):
    tokens, channels = queries.shape
    n_ctx = lax.axis_size("ctx")
    n_ch = lax.axis_size("ch")
    n_chip = n_ch // 2
    block = out_weight.shape[1] // n_ch
    width = channels // n_ctx
    per = tokens // BLOCK
    nb = n_ctx * per
    relay = n_chip == 4 and n_ctx == 4 and per == 4
    forward, backward = transform_tables(BLOCK)
    vmem = pl.BlockSpec(memory_space=pltpu.VMEM)
    hbm = pl.BlockSpec(memory_space=pl.ANY)
    dma = pltpu.SemaphoreType.DMA
    n_sub = tokens // SUB
    pieces = tokens // PIECE
    tiny = (16, 128)
    if relay:
        flows = [(tokens, block)] * 6 + [(tokens, channels)] * 2
        flow_sems = [(n_sub,)] * 10
        we_shape = (2, 2, channels, block)
    else:
        wide = (n_chip, tokens, block)
        flows = [wide, tiny, tiny, wide, wide, tiny, tiny, tiny]
        flow_sems = [(n_chip, per)] * 10
        we_shape = (2, 2, 16, 128)
    return pl.pallas_call(
        functools.partial(layer_kernel, n_ctx, n_ch, relay),
        out_shape=jax.ShapeDtypeStruct((tokens, block), BF16),
        in_specs=[hbm] * 4 + [vmem] + [hbm] * 3,
        out_specs=vmem,
        scratch_shapes=[
            pltpu.VMEM((tokens, channels), BF16),
            pltpu.VMEM((tokens, channels), BF16),
            pltpu.VMEM((tokens, channels), BF16),
            pltpu.VMEM((tokens, channels), BF16),
            pltpu.VMEM(forward.shape, BF16),
            pltpu.VMEM(backward.shape, BF16),
            pltpu.VMEM((n_chip, channels, block), BF16),
            pltpu.VMEM((n_chip, channels, block), BF16),
            pltpu.VMEM(we_shape, BF16),
            pltpu.VMEM((n_ctx, tokens, 2 * width), BF16),
            pltpu.VMEM((n_ctx, tokens, 2 * width), BF16),
            pltpu.VMEM((nb, 2 * BLOCK, 2 * width), F32),
            pltpu.VMEM((nb, 2 * BLOCK, width), F32),
            pltpu.VMEM((n_ctx, 2 * BLOCK, width), F32),
            pltpu.VMEM((n_ctx // 2, 2 * BLOCK, 2 * width), BF16),
            pltpu.VMEM((n_ctx // 2, 2 * BLOCK, 2 * width), BF16),
            pltpu.VMEM((n_ctx, tokens, width), BF16),
            pltpu.VMEM((n_ctx, tokens, width), BF16),
            pltpu.VMEM((tokens, channels), BF16),
            pltpu.VMEM((tokens, channels), BF16),
        ] + [pltpu.VMEM(shape, BF16) for shape in flows] + [
            pltpu.VMEM((tokens, block), F32),
            dma((3, per)), dma((3,)), dma((n_chip,)), dma((n_chip,)), dma((n_chip,)),
            dma((2, 2)), dma((2, 2)), dma((2,)),
            dma((n_ctx, per)), dma((n_ctx, per)), dma((n_ctx, pieces)), dma((n_ctx, pieces)),
            dma((pieces,)), dma((pieces,)),
        ] + [dma(shape) for shape in flow_sems],
        compiler_params=pltpu.CompilerParams(
            collective_id=0, has_side_effects=True, vmem_limit_bytes=VMEM_MIB * 1024 * 1024
        ),
        cost_estimate=pl.CostEstimate(
            flops=28 * n_ctx * tokens * BLOCK * width + 2 * tokens * channels * n_ch * block,
            bytes_accessed=12 * tokens * channels + 2 * channels * n_ch * block, transcendentals=0,
        ),
    )(queries, key_input, value_input, filters, skip_gain[None, :],
      jnp.asarray(forward), jnp.asarray(backward), out_weight)


def solution(mesh):
    in_specs = (
        P("ctx", "ch"),
        P("ctx", "ch"),
        P("ctx", "ch"),
        P("ctx", "ch"),
        P("ch"),
        P("ch", None),
    )
    return jax.shard_map(
        per_device, mesh=mesh, in_specs=in_specs, out_specs=P("ctx", "ch"), check_vma=False
    )
```

```python
import functools

import jax
import jax.numpy as jnp
import numpy as np
from jax import lax
from jax.experimental import pallas as pl
from jax.experimental.pallas import tpu as pltpu
from jax.sharding import PartitionSpec as P

BLOCK = 256
PIECE = 128
SUB = 64
WINDOW = 4
FINE = 1
AHEAD = 1
B_LAG = 4
VMEM_MIB = 56
F32 = jnp.float32
BF16 = jnp.bfloat16


def transform_tables(block):
    k = np.arange(block)[:, None]
    n = np.arange(block)[None, :]
    angle = np.pi * (((2 * k + 1) * n) % (4 * block)) / (2 * block)
    forward = np.concatenate([np.cos(angle), -np.sin(angle)], axis=0)
    backward = np.concatenate([np.cos(angle).T, -np.sin(angle).T], axis=1) / block

    def halves(table):
        high = table.astype(BF16)
        low = (table - high.astype(np.float64)).astype(BF16)
        return high, low

    f_high, f_low = halves(forward)
    b_high, b_low = halves(backward)
    return np.stack([f_high, f_low]), np.stack([b_high, b_low])


def dot(left, right):
    return jnp.dot(left, right, preferred_element_type=F32)


MESH = pl.DeviceIdType.MESH


def layer_kernel(n_ctx, n_ch, relay, q_hbm, k_hbm, v_hbm, h_hbm, skip_ref, f_hbm, b_hbm, w_hbm, out_hbm,
                 out_ref, out_sem, q_ref, k_ref, v_ref, h_ref, f_ref, b_ref, w_own, wx, we,
                 outbox, inbox, spec, zbuf, ybuf, yhigh, ylow, conv_out, conv_in, g_ref, gx,
                 send_a, send_b, send_c, recv_a, recv_b, recv_c, ge, gex, own,
                 load_sem, table_sem, w_sem, w_send, w_recv, we_send, we_recv, we_fwd,
                 in_send, in_recv, back_send, back_recv, g_send, g_recv,
                 a_send, a_recv, b_send, b_recv, c_send, c_recv, ge_send, ge_recv, gex_send, gex_recv):
    me = lax.axis_index("ctx")
    ch = lax.axis_index("ch")
    chip = lax.div(ch, 2)
    core = lax.rem(ch, 2)
    mate = ch + 1 - 2 * core
    n_chip = n_ch // 2
    tokens, block = out_ref.shape
    width = conv_in.shape[2]
    per = tokens // BLOCK
    halves = BLOCK // PIECE
    has_left = chip > 0
    has_right = chip < n_chip - 1
    left = jnp.maximum(ch - 2, core)
    right = jnp.minimum(ch + 2, n_ch - 2 + core)

    def remote(src, dst, sent, arrived, target):
        return pltpu.make_async_remote_copy(
            src_ref=src, dst_ref=dst, send_sem=sent, recv_sem=arrived,
            device_id=target, device_id_type=MESH,
        )

    def rows_of(r, size=BLOCK):
        return pl.ds(pl.multiple_of(r * size, size), size)

    barrier = pltpu.get_barrier_semaphore()

    def greet(target):
        pl.semaphore_signal(barrier, inc=1, device_id=target, device_id_type=MESH)

    greet({"ch": mate})
    for d in range(1, n_ctx):
        greet({"ctx": lax.rem(me + d, n_ctx)})

    @pl.when(has_left)
    def _():
        greet({"ch": left})
        greet({"ch": left + 1 - 2 * core})

    @pl.when(has_right)
    def _():
        greet({"ch": right})
        greet({"ch": right + 1 - 2 * core})

    def load(a, r):
        source, target = ((k_hbm, k_ref), (v_hbm, v_ref), (h_hbm, h_ref))[a]
        at = rows_of(r)
        return pltpu.make_async_copy(source.at[at], target.at[at], load_sem.at[a, r])

    f_load = pltpu.make_async_copy(f_hbm, f_ref, table_sem.at[0])
    b_load = pltpu.make_async_copy(b_hbm, b_ref, table_sem.at[1])
    q_load = pltpu.make_async_copy(q_hbm, q_ref, table_sem.at[2])

    def lanes_of(chip_at, core_at):
        return pl.ds(pl.multiple_of((chip_at * 2 + core_at) * block, block), block)

    def w_load(t):
        return pltpu.make_async_copy(w_hbm.at[:, lanes_of(t, core)], w_own.at[t], w_sem.at[t])

    def w_copy(t):
        return remote(w_hbm.at[:, lanes_of(t, 1 - core)], wx.at[t], w_send.at[t], w_recv.at[t], {"ch": mate})

    for r in range(per):
        for a in range(3):
            load(a, r).start()
    f_load.start()

    def in_copy(i, r):
        at = rows_of(r)
        return remote(outbox.at[i, at], inbox.at[me, at], in_send.at[i, r], in_recv.at[me, r], {"ctx": i})

    def in_arrival(i, r):
        at = rows_of(r)
        return remote(outbox.at[i, at], inbox.at[i, at], in_send.at[i, r], in_recv.at[i, r], {"ctx": i})

    pl.semaphore_wait(
        barrier, n_ctx + 2 * has_left.astype(jnp.int32) + 2 * has_right.astype(jnp.int32)
    )

    def fill(r, carry):
        for a in range(3):
            load(a, r).wait()
        at = rows_of(r)
        for i in range(n_ctx):
            lanes = slice(i * width, (i + 1) * width)
            mixed = k_ref[at, lanes].astype(F32) * v_ref[at, lanes].astype(F32)
            outbox[i, at, :width] = mixed.astype(BF16)
            outbox[i, at, width:] = h_ref[at, lanes]

            @pl.when(me != i)
            def _():
                in_copy(i, r).start()
        return carry

    lax.fori_loop(0, per, fill, 0)

    low = 1 - lax.div(chip, n_chip // 2)
    is_end = jnp.logical_or(chip == 0, chip == n_chip - 1)
    is_mid = jnp.logical_not(is_end)
    far = (n_chip - 1) * low
    end = (n_chip - 1) * (1 - low)
    across = n_chip - 1 - chip
    inner = 2 - low

    def bit_of(core_at):
        return (1 - core_at) * lax.rem(me, 2) + core_at * lax.div(me, 2)

    bit = bit_of(core)
    partner = (1 - core) * (me + 1 - 2 * lax.rem(me, 2)) + core * lax.rem(me + 2, 4)

    def we_copy(slot, core_at):
        column = inner * (1 - slot) + (n_chip - 1 - inner) * slot
        return remote(w_hbm.at[:, lanes_of(column, core_at)], we.at[slot, core],
                      we_send.at[slot, core_at], we_recv.at[slot, core], {"ch": inner * 2 + core_at})

    def we_arrival(slot, half):
        return remote(we.at[slot, half], we.at[slot, half], we_fwd.at[slot], we_recv.at[slot, half],
                      {"ctx": partner})

    if relay:
        for core_at in range(2):
            @pl.when(jnp.logical_and(is_end, bit_of(core_at) == core))
            def _():
                for slot in range(2):
                    we_copy(slot, core_at).start()

    b_load.start()
    q_load.start()
    for t in range(n_chip):
        w_load(t).start()
        w_copy(t).start()

    def ahead(box, source, r):
        data = box[source, rows_of(r), :]
        spec[source * per + r] = dot(f_ref[0], data) + dot(f_ref[1], data)

    f_load.wait()

    def ahead_own(r, carry):
        ahead(outbox, me, r)
        return carry

    lax.fori_loop(0, per, ahead_own, 0)

    def ahead_others(r, carry):
        for d in range(1, n_ctx):
            source = lax.rem(me + d, n_ctx)
            in_arrival(source, r).wait_recv()
            ahead(inbox, source, r)
        return carry

    nb = n_ctx * per
    rows = 8
    sign = 1.0 - 2.0 * (lax.broadcasted_iota(jnp.int32, (rows, width), 0) % 2).astype(F32)

    def parts_of(chunk):
        top = pl.multiple_of(chunk * rows, rows)
        return pl.ds(top, rows), pl.ds(pl.multiple_of(BLOCK + top, rows), rows)

    def is_last(p):
        return p % per == per - 1

    def sums(blocks, late, start, re, im):
        pairs = {j: [p for p in range(j + 1) if (is_last(p) or is_last(j - p)) == late] for j in blocks}
        used = {p for j in blocks for p in pairs[j]} | {j - p for j in blocks for p in pairs[j]}
        x = {p: (spec[p, re, :width], spec[p, im, :width]) for p in used}
        h = {p: (spec[p, re, width:], spec[p, im, width:]) for p in used}
        z = {}
        for j in blocks:
            zr, zi = start[j] if j in start else (None, None)
            for p in pairs[j]:
                xr, xi = x[p]
                hr, hi = h[j - p]
                tr = xr * hr - xi * hi
                ti = xr * hi + xi * hr
                zr = tr if zr is None else zr + tr
                zi = ti if zi is None else zi + ti
            z[j] = (zr, zi)
        return z

    def has_early(j):
        return any(not is_last(p) and not is_last(j - p) for p in range(j + 1))

    early = [j for j in range(nb) if has_early(j)]

    def early_sums(chunk, carry):
        re, im = parts_of(chunk)
        for j, (zr, zi) in sums(early, False, {}, re, im).items():
            zbuf[j, re, :] = zr
            zbuf[j, im, :] = zi
        return carry

    lax.fori_loop(0, per - 1, ahead_others, 0)
    lax.fori_loop(0, BLOCK // rows, early_sums, 0)
    ahead_others(per - 1, 0)
    b_load.wait()
    done = set()

    def products(m):
        mine = [i * per + m for i in range(n_ctx)]
        need = sorted(set(mine) | {j - 1 for j in mine if j > 0})
        fresh = [j for j in need if j not in done]
        done.update(fresh)

        def one(chunk, carry):
            re, im = parts_of(chunk)
            start = {j: (zbuf[j, re, :], zbuf[j, im, :]) for j in fresh if j in early}
            z = sums(fresh, True, start, re, im)
            for j in fresh:
                zbuf[j, re, :] = z[j][0]
                zbuf[j, im, :] = z[j][1]

            def get(j):
                return z[j] if j in z else (zbuf[j, re, :], zbuf[j, im, :])

            for i, j in enumerate(mine):
                yr, yi = get(j)
                if j > 0:
                    lr, li = get(j - 1)
                    yr = yr - sign * li
                    yi = yi + sign * lr
                ybuf[i, re, :] = yr
                ybuf[i, im, :] = yi
            return carry

        lax.fori_loop(0, BLOCK // rows, one, 0)
        for i in range(0, n_ctx, 2):
            data = jnp.concatenate([ybuf[i], ybuf[i + 1]], axis=1)
            high = data.astype(BF16)
            yhigh[i // 2] = high
            ylow[i // 2] = (data - high.astype(F32)).astype(BF16)

    def piece(m):
        return rows_of(m, PIECE)

    def back_copy(i, m):
        at = piece(m)
        return remote(conv_out.at[i, at], conv_in.at[me, at], back_send.at[i, m], back_recv.at[me, m], {"ctx": i})

    def back_arrival(i, m):
        at = piece(m)
        return remote(conv_out.at[i, at], conv_in.at[i, at], back_send.at[i, m], back_recv.at[i, m], {"ctx": i})

    def inverse(m):
        at = piece(m)
        inside = slice((m % halves) * PIECE, (m % halves + 1) * PIECE)
        b_high = b_ref[0, inside, :]
        b_low = b_ref[1, inside, :]
        for i in range(0, n_ctx, 2):
            high = yhigh[i // 2]
            conv = (dot(b_high, high) + (dot(b_high, ylow[i // 2]) + dot(b_low, high))).astype(BF16)
            for o in range(2):
                part = conv[:, o * width:(o + 1) * width]
                conv_out[i + o, at, :] = part

                @pl.when(me == i + o)
                def _():
                    conv_in[i + o, at, :] = part

                @pl.when(me != i + o)
                def _():
                    back_copy(i + o, m).start()

    def out_copy(m):
        at = piece(m)
        return pltpu.make_async_copy(out_ref.at[at], out_hbm.at[at], out_sem.at[m])

    def g_copy(m):
        at = piece(m)
        return remote(g_ref.at[at], gx.at[at], g_send.at[m], g_recv.at[m], {"ch": mate})

    def gate(m):
        at = piece(m)
        for i in range(n_ctx):
            @pl.when(me != i)
            def _():
                back_arrival(i, m).wait_recv()

        for i in range(n_ctx):
            lanes = slice(i * width, (i + 1) * width)
            mixed = outbox[i, at, :width].astype(F32)
            total = conv_in[i, at, :].astype(F32) + skip_ref[:, lanes] * mixed
            g_ref[at, lanes] = (q_ref[at, lanes].astype(F32) * total).astype(BF16)
        g_copy(m).start()

    def share(t, at):
        return dot(g_ref[at, :], w_own[t]) + dot(gx[at, :], wx[t])

    def weights_ready():
        for t in range(n_chip):
            w_load(t).wait()
            w_copy(t).wait()

    if relay:
        n_sub = tokens // SUB
        each = PIECE // SUB
        n_piece = tokens // PIECE
        to_inner = {"ch": inner * 2 + core}
        to_end = {"ch": end * 2 + core}
        to_across = {"ch": across * 2 + core}

        def sub(s):
            return rows_of(s, SUB)

        def a_from_end(s):
            return remote(send_a.at[sub(s)], recv_a.at[sub(s)], a_send.at[s], a_recv.at[s], to_inner)

        def a_from_mid(s):
            return remote(send_a.at[sub(s)], recv_b.at[sub(s)], a_send.at[s], b_recv.at[s], to_across)

        def b_from_mid(s):
            return remote(send_b.at[sub(s)], recv_b.at[sub(s)], b_send.at[s], b_recv.at[s], to_end)

        def a_arrival(s):
            return remote(send_a.at[sub(s)], recv_a.at[sub(s)], a_send.at[s], a_recv.at[s], to_end)

        def b_arrival(s):
            return remote(send_b.at[sub(s)], recv_b.at[sub(s)], b_send.at[s], b_recv.at[s], to_across)

        def c_copy(s):
            return remote(send_c.at[sub(s)], recv_c.at[sub(s)], c_send.at[s], c_recv.at[s], to_across)

        def ge_copy(s):
            return remote(g_ref.at[sub(s)], ge.at[sub(s)], ge_send.at[s], ge_recv.at[s], to_inner)

        def ge_arrival(s):
            return remote(g_ref.at[sub(s)], ge.at[sub(s)], ge_send.at[s], ge_recv.at[s], to_end)

        def gex_copy(s):
            return remote(ge.at[sub(s)], gex.at[sub(s)], gex_send.at[s], gex_recv.at[s], {"ch": mate})

        def end_first(m):
            @pl.when(is_end)
            def _():
                g_copy(m).wait()
                part = share(far, piece(m))
                for o in range(each):
                    s = m * each + o
                    send_a[sub(s), :] = part[o * SUB:(o + 1) * SUB].astype(BF16)
                    if s >= WINDOW:
                        a_from_end(s - WINDOW).wait_send()
                    a_from_end(s).start()

        def b_step(s):
            b_arrival(s).wait_recv()
            send_b[sub(s), :] = (own[sub(s), :] + recv_b[sub(s), :].astype(F32)).astype(BF16)
            b_from_mid(s).start()

        def mid_first(m):
            @pl.when(is_mid)
            def _():
                g_copy(m).wait()
                own[piece(m), :] = share(end, piece(m))
                part = share(far, piece(m))
                for o in range(each):
                    s = m * each + o
                    a_arrival(s).wait_recv()
                    send_a[sub(s), :] = (
                        part[o * SUB:(o + 1) * SUB] + recv_a[sub(s), :].astype(F32)
                    ).astype(BF16)
                    a_from_mid(s).start()
                    if s >= B_LAG:
                        b_step(s - B_LAG)

        def pass_weights():
            @pl.when(is_mid)
            def _():
                for slot in range(2):
                    we_arrival(slot, bit).wait_recv()
                    we_arrival(slot, bit).start()

        products(0)
        inverse(0)
        inverse(1)
        products(1)
        q_load.wait()
        gate(0)

        @pl.when(is_end)
        def _():
            for s in range(AHEAD):
                ge_copy(s).start()

        weights_ready()
        inverse(2)
        end_first(0)
        gate(1)
        inverse(3)
        end_first(1)
        products(2)
        gate(2)
        inverse(4)
        end_first(2)
        mid_first(0)
        gate(3)
        inverse(5)
        end_first(3)
        mid_first(1)
        products(3)
        inverse(6)
        inverse(7)
        pass_weights()
        for m in range(4, 8):
            gate(m)
            end_first(m)
            mid_first(m - 2)
        mid_first(6)
        mid_first(7)

        @pl.when(is_end)
        def _():
            for s in range(n_sub - WINDOW, n_sub):
                a_from_end(s).wait_send()

            def step(p, carry):
                for o in range(each):
                    s = p * each + o

                    @pl.when(s >= WINDOW)
                    def _():
                        ge_copy(s - WINDOW).wait_send()

                    @pl.when(s >= AHEAD)
                    def _():
                        ge_copy(s).start()

                at = piece(p)
                part = share(chip, at)
                for o in range(each):
                    b_arrival(p * each + o).wait_recv()
                out_ref[at, :] = (part + recv_b[at, :].astype(F32)).astype(BF16)
                out_copy(p).start()
                return carry

            lax.fori_loop(0, n_piece, step, 0)
            for s in range(n_sub - WINDOW, n_sub):
                ge_copy(s).wait_send()

        @pl.when(is_mid)
        def _():
            for slot in range(2):
                we_arrival(slot, 1 - bit).wait_recv()

            def finish(p):
                at = piece(p)
                for o in range(each):
                    c_copy(p * each + o).wait_recv()
                out_ref[at, :] = (own[at, :] + recv_c[at, :].astype(F32)).astype(BF16)
                out_copy(p).start()

            def relay_rows(at, subs):
                part = share(across, at)
                own_part = share(chip, at)
                for s in subs:
                    ge_arrival(s).wait_recv()
                    gex_copy(s).start()
                part += dot(ge[at, :], we[1, core])
                own_part += dot(ge[at, :], we[0, core])
                for s in subs:
                    gex_copy(s).wait_recv()
                send_c[at, :] = (part + dot(gex[at, :], we[1, 1 - core])).astype(BF16)
                for s in subs:
                    c_copy(s).start()
                own[at, :] = own_part + dot(gex[at, :], we[0, 1 - core])

            def step(p, carry):
                relay_rows(piece(p), [p * each + o for o in range(each)])

                @pl.when(p >= 2)
                def _():
                    finish(p - 2)
                return carry

            late = list(range(n_sub - B_LAG, n_sub))
            for s in range(each):
                relay_rows(sub(s), [s])
                if s > 0:
                    b_step(late.pop(0))
            for p in range(1, 3):
                relay_rows(piece(p), [p * each + o for o in range(each)])
                for s in late[:2]:
                    b_step(s)
                late = late[2:]
            for s in late:
                b_step(s)
            finish(0)
            lax.fori_loop(3, n_piece - FINE, step, 0)
            finish(n_piece - FINE - 2)
            for s in range((n_piece - FINE) * each, n_sub):
                relay_rows(sub(s), [s])
            for p in range(n_piece - FINE - 1, n_piece):
                finish(p)

            def drain(s, carry):
                a_from_mid(s).wait_send()
                b_from_mid(s).wait_send()
                c_copy(s).wait_send()
                gex_copy(s).wait_send()
                return carry

            lax.fori_loop(0, n_sub, drain, 0)
            for slot in range(2):
                we_arrival(slot, bit).wait_send()

        for core_at in range(2):
            @pl.when(jnp.logical_and(is_end, bit_of(core_at) == core))
            def _():
                for slot in range(2):
                    we_copy(slot, core_at).wait_send()
    else:
        def to_right(t, m):
            at = rows_of(m)
            return remote(send_a.at[t, at], recv_a.at[t, at], a_send.at[t, m], a_recv.at[t, m], {"ch": right})

        def to_left(t, m):
            at = rows_of(m)
            return remote(send_a.at[t, at], recv_b.at[t, at], a_send.at[t, m], b_recv.at[t, m], {"ch": left})

        def arrive_left(t, m):
            at = rows_of(m)
            return remote(send_a.at[t, at], recv_a.at[t, at], a_send.at[t, m], a_recv.at[t, m], {"ch": left})

        def arrive_right(t, m):
            at = rows_of(m)
            return remote(send_a.at[t, at], recv_b.at[t, at], a_send.at[t, m], b_recv.at[t, m], {"ch": right})

        def pass_on(t, m, first, arrived, buffer, copy):
            at = rows_of(m)
            part = share(t, at)

            @pl.when(first)
            def _():
                send_a[t, at, :] = part.astype(BF16)

            @pl.when(jnp.logical_not(first))
            def _():
                arrived(t, m).wait_recv()
                send_a[t, at, :] = (part + buffer[t, at, :].astype(F32)).astype(BF16)

            copy(t, m).start()

        def step(m, carry):
            for o in range(halves):
                g_copy(m * halves + o).wait()
            for d in range(n_chip - 1, 0, -1):
                @pl.when(chip + d < n_chip)
                def _():
                    pass_on(chip + d, m, jnp.logical_not(has_left), arrive_left, recv_a, to_right)

                @pl.when(chip - d >= 0)
                def _():
                    pass_on(chip - d, m, jnp.logical_not(has_right), arrive_right, recv_b, to_left)

            own[rows_of(m), :] = share(chip, rows_of(m))
            return carry

        def finish(m, carry):
            at = rows_of(m)

            @pl.when(has_left)
            def _():
                arrive_left(chip, m).wait_recv()
                own[at, :] += recv_a[chip, at, :].astype(F32)

            @pl.when(has_right)
            def _():
                arrive_right(chip, m).wait_recv()
                own[at, :] += recv_b[chip, at, :].astype(F32)

            out_ref[at, :] = own[at, :].astype(BF16)
            for o in range(halves):
                out_copy(m * halves + o).start()
            for d in range(n_chip - 1, 0, -1):
                @pl.when(chip + d < n_chip)
                def _():
                    to_right(chip + d, m).wait_send()

                @pl.when(chip - d >= 0)
                def _():
                    to_left(chip - d, m).wait_send()
            return carry

        q_load.wait()
        for m in range(per):
            products(m)
            for o in range(halves):
                inverse(m * halves + o)
            if m > 0:
                for o in range(halves):
                    gate((m - 1) * halves + o)
        for o in range(halves):
            gate((per - 1) * halves + o)
        weights_ready()
        lax.fori_loop(0, per, step, 0)
        lax.fori_loop(0, per, finish, 0)

    def drain_ctx(r, carry):
        for i in range(n_ctx):
            @pl.when(me != i)
            def _():
                in_copy(i, r).wait_send()
                for o in range(halves):
                    back_copy(i, r * halves + o).wait_send()
        return carry

    lax.fori_loop(0, per, drain_ctx, 0)

    def drain_out(m, carry):
        out_copy(m).wait()
        return carry

    lax.fori_loop(0, tokens // PIECE, drain_out, 0)


def per_device(queries, key_input, value_input, filters, skip_gain, out_weight):
    tokens, channels = queries.shape
    n_ctx = lax.axis_size("ctx")
    n_ch = lax.axis_size("ch")
    n_chip = n_ch // 2
    block = out_weight.shape[1] // n_ch
    width = channels // n_ctx
    per = tokens // BLOCK
    nb = n_ctx * per
    relay = n_chip == 4 and n_ctx == 4 and per == 4
    forward, backward = transform_tables(BLOCK)
    vmem = pl.BlockSpec(memory_space=pltpu.VMEM)
    hbm = pl.BlockSpec(memory_space=pl.ANY)
    dma = pltpu.SemaphoreType.DMA
    n_sub = tokens // SUB
    pieces = tokens // PIECE
    tiny = (16, 128)
    if relay:
        flows = [(tokens, block)] * 6 + [(tokens, channels)] * 2
        flow_sems = [(n_sub,)] * 10
        we_shape = (2, 2, channels, block)
    else:
        wide = (n_chip, tokens, block)
        flows = [wide, tiny, tiny, wide, wide, tiny, tiny, tiny]
        flow_sems = [(n_chip, per)] * 10
        we_shape = (2, 2, 16, 128)
    return pl.pallas_call(
        functools.partial(layer_kernel, n_ctx, n_ch, relay),
        out_shape=jax.ShapeDtypeStruct((tokens, block), BF16),
        in_specs=[hbm] * 4 + [vmem] + [hbm] * 3,
        out_specs=hbm,
        scratch_shapes=[
            pltpu.VMEM((tokens, block), BF16),
            dma((pieces,)),
            pltpu.VMEM((tokens, channels), BF16),
            pltpu.VMEM((tokens, channels), BF16),
            pltpu.VMEM((tokens, channels), BF16),
            pltpu.VMEM((tokens, channels), BF16),
            pltpu.VMEM(forward.shape, BF16),
            pltpu.VMEM(backward.shape, BF16),
            pltpu.VMEM((n_chip, channels, block), BF16),
            pltpu.VMEM((n_chip, channels, block), BF16),
            pltpu.VMEM(we_shape, BF16),
            pltpu.VMEM((n_ctx, tokens, 2 * width), BF16),
            pltpu.VMEM((n_ctx, tokens, 2 * width), BF16),
            pltpu.VMEM((nb, 2 * BLOCK, 2 * width), F32),
            pltpu.VMEM((nb, 2 * BLOCK, width), F32),
            pltpu.VMEM((n_ctx, 2 * BLOCK, width), F32),
            pltpu.VMEM((n_ctx // 2, 2 * BLOCK, 2 * width), BF16),
            pltpu.VMEM((n_ctx // 2, 2 * BLOCK, 2 * width), BF16),
            pltpu.VMEM((n_ctx, tokens, width), BF16),
            pltpu.VMEM((n_ctx, tokens, width), BF16),
            pltpu.VMEM((tokens, channels), BF16),
            pltpu.VMEM((tokens, channels), BF16),
        ] + [pltpu.VMEM(shape, BF16) for shape in flows] + [
            pltpu.VMEM((tokens, block), F32),
            dma((3, per)), dma((3,)), dma((n_chip,)), dma((n_chip,)), dma((n_chip,)),
            dma((2, 2)), dma((2, 2)), dma((2,)),
            dma((n_ctx, per)), dma((n_ctx, per)), dma((n_ctx, pieces)), dma((n_ctx, pieces)),
            dma((pieces,)), dma((pieces,)),
        ] + [dma(shape) for shape in flow_sems],
        compiler_params=pltpu.CompilerParams(
            collective_id=0, has_side_effects=True, vmem_limit_bytes=VMEM_MIB * 1024 * 1024
        ),
        cost_estimate=pl.CostEstimate(
            flops=28 * n_ctx * tokens * BLOCK * width + 2 * tokens * channels * n_ch * block,
            bytes_accessed=12 * tokens * channels + 2 * channels * n_ch * block, transcendentals=0,
        ),
    )(queries, key_input, value_input, filters, skip_gain[None, :],
      jnp.asarray(forward), jnp.asarray(backward), out_weight)


def solution(mesh):
    in_specs = (
        P("ctx", "ch"),
        P("ctx", "ch"),
        P("ctx", "ch"),
        P("ctx", "ch"),
        P("ch"),
        P("ch", None),
    )
    return jax.shard_map(
        per_device, mesh=mesh, in_specs=in_specs, out_specs=P("ctx", "ch"), check_vma=False
    )
```

```python
import functools

import jax
import jax.numpy as jnp
import numpy as np
from jax import lax
from jax.experimental import pallas as pl
from jax.experimental.pallas import tpu as pltpu
from jax.sharding import PartitionSpec as P

BLOCK = 256
PIECE = 128
SUB = 64
WINDOW = 4
AHEAD = 2
B_LAG = 4
VMEM_MIB = 56
F32 = jnp.float32
BF16 = jnp.bfloat16


def transform_tables(block):
    k = np.arange(block)[:, None]
    n = np.arange(block)[None, :]
    angle = np.pi * (((2 * k + 1) * n) % (4 * block)) / (2 * block)
    forward = np.concatenate([np.cos(angle), -np.sin(angle)], axis=0)
    backward = np.concatenate([np.cos(angle).T, -np.sin(angle).T], axis=1) / block

    def halves(table):
        high = table.astype(BF16)
        low = (table - high.astype(np.float64)).astype(BF16)
        return high, low

    f_high, f_low = halves(forward)
    b_high, b_low = halves(backward)
    return np.stack([f_high, f_low]), np.stack([b_high, b_low])


def dot(left, right):
    return jnp.dot(left, right, preferred_element_type=F32)


MESH = pl.DeviceIdType.MESH


def layer_kernel(n_ctx, n_ch, relay, q_hbm, k_hbm, v_hbm, h_hbm, skip_ref, f_hbm, b_hbm, w_hbm, out_hbm,
                 out_ref, out_sem, q_ref, k_ref, v_ref, h_ref, f_ref, b_ref, w_own, wx, we,
                 outbox, inbox, spec, zbuf, ybuf, yhigh, ylow, conv_out, conv_in, g_ref, gx,
                 send_a, send_b, send_c, recv_a, recv_b, recv_c, ge, gex, own, ahead_c,
                 load_sem, table_sem, w_sem, w_send, w_recv, we_send, we_recv, we_fwd,
                 in_send, in_recv, back_send, back_recv, g_send, g_recv,
                 a_send, a_recv, b_send, b_recv, c_send, c_recv, ge_send, ge_recv, gex_send, gex_recv):
    me = lax.axis_index("ctx")
    ch = lax.axis_index("ch")
    chip = lax.div(ch, 2)
    core = lax.rem(ch, 2)
    mate = ch + 1 - 2 * core
    n_chip = n_ch // 2
    tokens, block = out_ref.shape
    width = conv_in.shape[2]
    per = tokens // BLOCK
    halves = BLOCK // PIECE
    has_left = chip > 0
    has_right = chip < n_chip - 1
    left = jnp.maximum(ch - 2, core)
    right = jnp.minimum(ch + 2, n_ch - 2 + core)

    def remote(src, dst, sent, arrived, target):
        return pltpu.make_async_remote_copy(
            src_ref=src, dst_ref=dst, send_sem=sent, recv_sem=arrived,
            device_id=target, device_id_type=MESH,
        )

    def rows_of(r, size=BLOCK):
        return pl.ds(pl.multiple_of(r * size, size), size)

    barrier = pltpu.get_barrier_semaphore()

    def greet(target):
        pl.semaphore_signal(barrier, inc=1, device_id=target, device_id_type=MESH)

    greet({"ch": mate})
    for d in range(1, n_ctx):
        greet({"ctx": lax.rem(me + d, n_ctx)})

    @pl.when(has_left)
    def _():
        greet({"ch": left})
        greet({"ch": left + 1 - 2 * core})

    @pl.when(has_right)
    def _():
        greet({"ch": right})
        greet({"ch": right + 1 - 2 * core})

    def load(a, r):
        source, target = ((k_hbm, k_ref), (v_hbm, v_ref), (h_hbm, h_ref))[a]
        at = rows_of(r)
        return pltpu.make_async_copy(source.at[at], target.at[at], load_sem.at[a, r])

    f_load = pltpu.make_async_copy(f_hbm, f_ref, table_sem.at[0])
    b_load = pltpu.make_async_copy(b_hbm, b_ref, table_sem.at[1])
    q_load = pltpu.make_async_copy(q_hbm, q_ref, table_sem.at[2])

    def lanes_of(chip_at, core_at):
        return pl.ds(pl.multiple_of((chip_at * 2 + core_at) * block, block), block)

    def w_load(t):
        return pltpu.make_async_copy(w_hbm.at[:, lanes_of(t, core)], w_own.at[t], w_sem.at[t])

    def w_copy(t):
        return remote(w_hbm.at[:, lanes_of(t, 1 - core)], wx.at[t], w_send.at[t], w_recv.at[t], {"ch": mate})

    for r in range(per):
        for a in range(3):
            load(a, r).start()
    f_load.start()

    def in_copy(i, r):
        at = rows_of(r)
        return remote(outbox.at[i, at], inbox.at[me, at], in_send.at[i, r], in_recv.at[me, r], {"ctx": i})

    def in_arrival(i, r):
        at = rows_of(r)
        return remote(outbox.at[i, at], inbox.at[i, at], in_send.at[i, r], in_recv.at[i, r], {"ctx": i})

    pl.semaphore_wait(
        barrier, n_ctx + 2 * has_left.astype(jnp.int32) + 2 * has_right.astype(jnp.int32)
    )

    def fill(r, carry):
        for a in range(3):
            load(a, r).wait()
        at = rows_of(r)
        for i in range(n_ctx):
            lanes = slice(i * width, (i + 1) * width)
            mixed = k_ref[at, lanes].astype(F32) * v_ref[at, lanes].astype(F32)
            outbox[i, at, :width] = mixed.astype(BF16)
            outbox[i, at, width:] = h_ref[at, lanes]

            @pl.when(me != i)
            def _():
                in_copy(i, r).start()
        return carry

    lax.fori_loop(0, per, fill, 0)

    low = 1 - lax.div(chip, n_chip // 2)
    is_end = jnp.logical_or(chip == 0, chip == n_chip - 1)
    is_mid = jnp.logical_not(is_end)
    far = (n_chip - 1) * low
    end = (n_chip - 1) * (1 - low)
    across = n_chip - 1 - chip
    inner = 2 - low

    def bit_of(core_at):
        return (1 - core_at) * lax.rem(me, 2) + core_at * lax.div(me, 2)

    bit = bit_of(core)
    partner = (1 - core) * (me + 1 - 2 * lax.rem(me, 2)) + core * lax.rem(me + 2, 4)

    def we_copy(slot, core_at):
        column = inner * (1 - slot) + (n_chip - 1 - inner) * slot
        return remote(w_hbm.at[:, lanes_of(column, core_at)], we.at[slot, core],
                      we_send.at[slot, core_at], we_recv.at[slot, core], {"ch": inner * 2 + core_at})

    def we_arrival(slot, half):
        return remote(we.at[slot, half], we.at[slot, half], we_fwd.at[slot], we_recv.at[slot, half],
                      {"ctx": partner})

    if relay:
        for core_at in range(2):
            @pl.when(jnp.logical_and(is_end, bit_of(core_at) == core))
            def _():
                for slot in range(2):
                    we_copy(slot, core_at).start()

    b_load.start()
    q_load.start()
    for t in range(n_chip):
        w_load(t).start()
        w_copy(t).start()

    def ahead(box, source, r):
        data = box[source, rows_of(r), :]
        spec[source * per + r] = dot(f_ref[0], data) + dot(f_ref[1], data)

    f_load.wait()

    def ahead_own(r, carry):
        ahead(outbox, me, r)
        return carry

    lax.fori_loop(0, per, ahead_own, 0)

    def ahead_others(r, carry):
        for d in range(1, n_ctx):
            source = lax.rem(me + d, n_ctx)
            in_arrival(source, r).wait_recv()
            ahead(inbox, source, r)
        return carry

    nb = n_ctx * per
    rows = 8
    sign = 1.0 - 2.0 * (lax.broadcasted_iota(jnp.int32, (rows, width), 0) % 2).astype(F32)

    def parts_of(chunk):
        top = pl.multiple_of(chunk * rows, rows)
        return pl.ds(top, rows), pl.ds(pl.multiple_of(BLOCK + top, rows), rows)

    def is_last(p):
        return p % per == per - 1

    def sums(blocks, late, start, re, im):
        pairs = {j: [p for p in range(j + 1) if (is_last(p) or is_last(j - p)) == late] for j in blocks}
        used = {p for j in blocks for p in pairs[j]} | {j - p for j in blocks for p in pairs[j]}
        x = {p: (spec[p, re, :width], spec[p, im, :width]) for p in used}
        h = {p: (spec[p, re, width:], spec[p, im, width:]) for p in used}
        z = {}
        for j in blocks:
            zr, zi = start[j] if j in start else (None, None)
            for p in pairs[j]:
                xr, xi = x[p]
                hr, hi = h[j - p]
                tr = xr * hr - xi * hi
                ti = xr * hi + xi * hr
                zr = tr if zr is None else zr + tr
                zi = ti if zi is None else zi + ti
            z[j] = (zr, zi)
        return z

    def has_early(j):
        return any(not is_last(p) and not is_last(j - p) for p in range(j + 1))

    early = [j for j in range(nb) if has_early(j)]

    def early_sums(chunk, carry):
        re, im = parts_of(chunk)
        for j, (zr, zi) in sums(early, False, {}, re, im).items():
            zbuf[j, re, :] = zr
            zbuf[j, im, :] = zi
        return carry

    lax.fori_loop(0, per - 1, ahead_others, 0)
    lax.fori_loop(0, BLOCK // rows, early_sums, 0)
    ahead_others(per - 1, 0)
    b_load.wait()
    done = set()

    def products(m):
        mine = [i * per + m for i in range(n_ctx)]
        need = sorted(set(mine) | {j - 1 for j in mine if j > 0})
        fresh = [j for j in need if j not in done]
        done.update(fresh)

        def one(chunk, carry):
            re, im = parts_of(chunk)
            start = {j: (zbuf[j, re, :], zbuf[j, im, :]) for j in fresh if j in early}
            z = sums(fresh, True, start, re, im)
            for j in fresh:
                zbuf[j, re, :] = z[j][0]
                zbuf[j, im, :] = z[j][1]

            def get(j):
                return z[j] if j in z else (zbuf[j, re, :], zbuf[j, im, :])

            for i, j in enumerate(mine):
                yr, yi = get(j)
                if j > 0:
                    lr, li = get(j - 1)
                    yr = yr - sign * li
                    yi = yi + sign * lr
                ybuf[i, re, :] = yr
                ybuf[i, im, :] = yi
            return carry

        lax.fori_loop(0, BLOCK // rows, one, 0)
        for i in range(0, n_ctx, 2):
            data = jnp.concatenate([ybuf[i], ybuf[i + 1]], axis=1)
            high = data.astype(BF16)
            yhigh[i // 2] = high
            ylow[i // 2] = (data - high.astype(F32)).astype(BF16)

    def piece(m):
        return rows_of(m, PIECE)

    def back_copy(i, m):
        at = piece(m)
        return remote(conv_out.at[i, at], conv_in.at[me, at], back_send.at[i, m], back_recv.at[me, m], {"ctx": i})

    def back_arrival(i, m):
        at = piece(m)
        return remote(conv_out.at[i, at], conv_in.at[i, at], back_send.at[i, m], back_recv.at[i, m], {"ctx": i})

    def inverse(m):
        at = piece(m)
        inside = slice((m % halves) * PIECE, (m % halves + 1) * PIECE)
        b_high = b_ref[0, inside, :]
        b_low = b_ref[1, inside, :]
        for i in range(0, n_ctx, 2):
            high = yhigh[i // 2]
            conv = (dot(b_high, high) + (dot(b_high, ylow[i // 2]) + dot(b_low, high))).astype(BF16)
            for o in range(2):
                part = conv[:, o * width:(o + 1) * width]
                conv_out[i + o, at, :] = part

                @pl.when(me == i + o)
                def _():
                    conv_in[i + o, at, :] = part

                @pl.when(me != i + o)
                def _():
                    back_copy(i + o, m).start()

    def out_copy(m):
        at = piece(m)
        return pltpu.make_async_copy(out_ref.at[at], out_hbm.at[at], out_sem.at[m])

    def g_copy(m):
        at = piece(m)
        return remote(g_ref.at[at], gx.at[at], g_send.at[m], g_recv.at[m], {"ch": mate})

    def gate(m):
        at = piece(m)
        for i in range(n_ctx):
            @pl.when(me != i)
            def _():
                back_arrival(i, m).wait_recv()

        for i in range(n_ctx):
            lanes = slice(i * width, (i + 1) * width)
            mixed = outbox[i, at, :width].astype(F32)
            total = conv_in[i, at, :].astype(F32) + skip_ref[:, lanes] * mixed
            g_ref[at, lanes] = (q_ref[at, lanes].astype(F32) * total).astype(BF16)
        g_copy(m).start()

    def share(t, at):
        return dot(g_ref[at, :], w_own[t]) + dot(gx[at, :], wx[t])

    def weights_ready():
        for t in range(n_chip):
            w_load(t).wait()
            w_copy(t).wait()

    if relay:
        n_sub = tokens // SUB
        each = PIECE // SUB
        n_piece = tokens // PIECE
        to_inner = {"ch": inner * 2 + core}
        to_end = {"ch": end * 2 + core}
        to_across = {"ch": across * 2 + core}

        def sub(s):
            return rows_of(s, SUB)

        def a_from_end(s):
            return remote(send_a.at[sub(s)], recv_a.at[sub(s)], a_send.at[s], a_recv.at[s], to_inner)

        def a_from_mid(s):
            return remote(send_a.at[sub(s)], recv_b.at[sub(s)], a_send.at[s], b_recv.at[s], to_across)

        def b_from_mid(s):
            return remote(send_b.at[sub(s)], recv_b.at[sub(s)], b_send.at[s], b_recv.at[s], to_end)

        def a_arrival(s):
            return remote(send_a.at[sub(s)], recv_a.at[sub(s)], a_send.at[s], a_recv.at[s], to_end)

        def b_arrival(s):
            return remote(send_b.at[sub(s)], recv_b.at[sub(s)], b_send.at[s], b_recv.at[s], to_across)

        def c_copy(s):
            return remote(send_c.at[sub(s)], recv_c.at[sub(s)], c_send.at[s], c_recv.at[s], to_across)

        def ge_copy(s):
            return remote(g_ref.at[sub(s)], ge.at[sub(s)], ge_send.at[s], ge_recv.at[s], to_inner)

        def ge_arrival(s):
            return remote(g_ref.at[sub(s)], ge.at[sub(s)], ge_send.at[s], ge_recv.at[s], to_end)

        def gex_copy(s):
            return remote(ge.at[sub(s)], gex.at[sub(s)], gex_send.at[s], gex_recv.at[s], {"ch": mate})

        def end_first(m):
            @pl.when(is_end)
            def _():
                g_copy(m).wait()
                part = share(far, piece(m))
                for o in range(each):
                    s = m * each + o
                    send_a[sub(s), :] = part[o * SUB:(o + 1) * SUB].astype(BF16)
                    if s >= WINDOW:
                        a_from_end(s - WINDOW).wait_send()
                    a_from_end(s).start()

        def b_step(s):
            b_arrival(s).wait_recv()
            send_b[sub(s), :] = (own[sub(s), :] + recv_b[sub(s), :].astype(F32)).astype(BF16)
            b_from_mid(s).start()

        def mid_first(m):
            @pl.when(is_mid)
            def _():
                g_copy(m).wait()
                own[piece(m), :] = share(end, piece(m))
                part = share(far, piece(m))
                for o in range(each):
                    s = m * each + o
                    a_arrival(s).wait_recv()
                    send_a[sub(s), :] = (
                        part[o * SUB:(o + 1) * SUB] + recv_a[sub(s), :].astype(F32)
                    ).astype(BF16)
                    a_from_mid(s).start()
                    if s >= B_LAG:
                        b_step(s - B_LAG)

        def pass_weights():
            @pl.when(is_mid)
            def _():
                for slot in range(2):
                    we_arrival(slot, bit).wait_recv()
                    we_arrival(slot, bit).start()

        products(0)
        inverse(0)
        inverse(1)
        products(1)
        q_load.wait()
        gate(0)

        @pl.when(is_end)
        def _():
            for s in range(AHEAD):
                ge_copy(s).start()

        weights_ready()
        inverse(2)
        end_first(0)
        gate(1)
        inverse(3)
        end_first(1)
        products(2)
        gate(2)
        inverse(4)
        end_first(2)
        mid_first(0)
        gate(3)
        inverse(5)
        end_first(3)
        mid_first(1)
        products(3)
        inverse(6)
        inverse(7)
        pass_weights()
        for m in range(4, 8):
            gate(m)
            end_first(m)
            mid_first(m - 2)
        mid_first(6)

        def own_shares(p):
            at = piece(p)
            ahead_c[at, :] = share(across, at)
            own[at, :] = share(chip, at)

        @pl.when(is_mid)
        def _():
            own_shares(0)

        mid_first(7)

        @pl.when(is_end)
        def _():
            for s in range(n_sub - WINDOW, n_sub):
                a_from_end(s).wait_send()

            def step(p, carry):
                for o in range(each):
                    s = p * each + o

                    @pl.when(s >= WINDOW)
                    def _():
                        ge_copy(s - WINDOW).wait_send()

                    @pl.when(s >= AHEAD)
                    def _():
                        ge_copy(s).start()

                at = piece(p)
                part = share(chip, at)
                for o in range(each):
                    b_arrival(p * each + o).wait_recv()
                out_ref[at, :] = (part + recv_b[at, :].astype(F32)).astype(BF16)
                out_copy(p).start()
                return carry

            lax.fori_loop(0, n_piece, step, 0)
            for s in range(n_sub - WINDOW, n_sub):
                ge_copy(s).wait_send()

        @pl.when(is_mid)
        def _():
            for slot in range(2):
                we_arrival(slot, 1 - bit).wait_recv()

            def finish(p):
                at = piece(p)
                for o in range(each):
                    c_copy(p * each + o).wait_recv()
                out_ref[at, :] = (own[at, :] + recv_c[at, :].astype(F32)).astype(BF16)
                out_copy(p).start()

            def relay_rows(at, subs, between):
                for s in subs:
                    ge_arrival(s).wait_recv()
                    gex_copy(s).start()
                part = ahead_c[at, :] + dot(ge[at, :], we[1, core])
                own[at, :] += dot(ge[at, :], we[0, core])
                between()
                for s in subs:
                    gex_copy(s).wait_recv()
                send_c[at, :] = (part + dot(gex[at, :], we[1, 1 - core])).astype(BF16)
                for s in subs:
                    c_copy(s).start()
                own[at, :] += dot(gex[at, :], we[0, 1 - core])

            def relay_piece(p, between):
                relay_rows(piece(p), [p * each + o for o in range(each)], between)

            def nothing():
                pass

            late = list(range(n_sub - B_LAG, n_sub))
            for s in range(each):
                relay_rows(sub(s), [s], (lambda: own_shares(1)) if s == each - 1 else nothing)
                if s > 0:
                    b_step(late.pop(0))
            for p in range(1, 3):
                relay_piece(p, functools.partial(own_shares, p + 1))
                for s in late[:2]:
                    b_step(s)
                late = late[2:]
            for s in late:
                b_step(s)

            def step(p, carry):
                def between():
                    own_shares(p + 1)
                    finish(p - 3)

                relay_piece(p, between)
                return carry

            lax.fori_loop(3, n_piece - 1, step, 0)
            for s in range(n_sub - each, n_sub):
                relay_rows(sub(s), [s], (lambda: finish(n_piece - 4)) if s == n_sub - each else nothing)
            for p in range(n_piece - 3, n_piece):
                finish(p)

            def drain(s, carry):
                a_from_mid(s).wait_send()
                b_from_mid(s).wait_send()
                c_copy(s).wait_send()
                gex_copy(s).wait_send()
                return carry

            lax.fori_loop(0, n_sub, drain, 0)
            for slot in range(2):
                we_arrival(slot, bit).wait_send()

        for core_at in range(2):
            @pl.when(jnp.logical_and(is_end, bit_of(core_at) == core))
            def _():
                for slot in range(2):
                    we_copy(slot, core_at).wait_send()
    else:
        def to_right(t, m):
            at = rows_of(m)
            return remote(send_a.at[t, at], recv_a.at[t, at], a_send.at[t, m], a_recv.at[t, m], {"ch": right})

        def to_left(t, m):
            at = rows_of(m)
            return remote(send_a.at[t, at], recv_b.at[t, at], a_send.at[t, m], b_recv.at[t, m], {"ch": left})

        def arrive_left(t, m):
            at = rows_of(m)
            return remote(send_a.at[t, at], recv_a.at[t, at], a_send.at[t, m], a_recv.at[t, m], {"ch": left})

        def arrive_right(t, m):
            at = rows_of(m)
            return remote(send_a.at[t, at], recv_b.at[t, at], a_send.at[t, m], b_recv.at[t, m], {"ch": right})

        def pass_on(t, m, first, arrived, buffer, copy):
            at = rows_of(m)
            part = share(t, at)

            @pl.when(first)
            def _():
                send_a[t, at, :] = part.astype(BF16)

            @pl.when(jnp.logical_not(first))
            def _():
                arrived(t, m).wait_recv()
                send_a[t, at, :] = (part + buffer[t, at, :].astype(F32)).astype(BF16)

            copy(t, m).start()

        def step(m, carry):
            for o in range(halves):
                g_copy(m * halves + o).wait()
            for d in range(n_chip - 1, 0, -1):
                @pl.when(chip + d < n_chip)
                def _():
                    pass_on(chip + d, m, jnp.logical_not(has_left), arrive_left, recv_a, to_right)

                @pl.when(chip - d >= 0)
                def _():
                    pass_on(chip - d, m, jnp.logical_not(has_right), arrive_right, recv_b, to_left)

            own[rows_of(m), :] = share(chip, rows_of(m))
            return carry

        def finish(m, carry):
            at = rows_of(m)

            @pl.when(has_left)
            def _():
                arrive_left(chip, m).wait_recv()
                own[at, :] += recv_a[chip, at, :].astype(F32)

            @pl.when(has_right)
            def _():
                arrive_right(chip, m).wait_recv()
                own[at, :] += recv_b[chip, at, :].astype(F32)

            out_ref[at, :] = own[at, :].astype(BF16)
            for o in range(halves):
                out_copy(m * halves + o).start()
            for d in range(n_chip - 1, 0, -1):
                @pl.when(chip + d < n_chip)
                def _():
                    to_right(chip + d, m).wait_send()

                @pl.when(chip - d >= 0)
                def _():
                    to_left(chip - d, m).wait_send()
            return carry

        q_load.wait()
        for m in range(per):
            products(m)
            for o in range(halves):
                inverse(m * halves + o)
            if m > 0:
                for o in range(halves):
                    gate((m - 1) * halves + o)
        for o in range(halves):
            gate((per - 1) * halves + o)
        weights_ready()
        lax.fori_loop(0, per, step, 0)
        lax.fori_loop(0, per, finish, 0)

    def drain_ctx(r, carry):
        for i in range(n_ctx):
            @pl.when(me != i)
            def _():
                in_copy(i, r).wait_send()
                for o in range(halves):
                    back_copy(i, r * halves + o).wait_send()
        return carry

    lax.fori_loop(0, per, drain_ctx, 0)

    def drain_out(m, carry):
        out_copy(m).wait()
        return carry

    lax.fori_loop(0, tokens // PIECE, drain_out, 0)


def per_device(queries, key_input, value_input, filters, skip_gain, out_weight):
    tokens, channels = queries.shape
    n_ctx = lax.axis_size("ctx")
    n_ch = lax.axis_size("ch")
    n_chip = n_ch // 2
    block = out_weight.shape[1] // n_ch
    width = channels // n_ctx
    per = tokens // BLOCK
    nb = n_ctx * per
    relay = n_chip == 4 and n_ctx == 4 and per == 4
    forward, backward = transform_tables(BLOCK)
    vmem = pl.BlockSpec(memory_space=pltpu.VMEM)
    hbm = pl.BlockSpec(memory_space=pl.ANY)
    dma = pltpu.SemaphoreType.DMA
    n_sub = tokens // SUB
    pieces = tokens // PIECE
    tiny = (16, 128)
    if relay:
        flows = [(tokens, block)] * 6 + [(tokens, channels)] * 2
        flow_sems = [(n_sub,)] * 10
        we_shape = (2, 2, channels, block)
    else:
        wide = (n_chip, tokens, block)
        flows = [wide, tiny, tiny, wide, wide, tiny, tiny, tiny]
        flow_sems = [(n_chip, per)] * 10
        we_shape = (2, 2, 16, 128)
    return pl.pallas_call(
        functools.partial(layer_kernel, n_ctx, n_ch, relay),
        out_shape=jax.ShapeDtypeStruct((tokens, block), BF16),
        in_specs=[hbm] * 4 + [vmem] + [hbm] * 3,
        out_specs=hbm,
        scratch_shapes=[
            pltpu.VMEM((tokens, block), BF16),
            dma((pieces,)),
            pltpu.VMEM((tokens, channels), BF16),
            pltpu.VMEM((tokens, channels), BF16),
            pltpu.VMEM((tokens, channels), BF16),
            pltpu.VMEM((tokens, channels), BF16),
            pltpu.VMEM(forward.shape, BF16),
            pltpu.VMEM(backward.shape, BF16),
            pltpu.VMEM((n_chip, channels, block), BF16),
            pltpu.VMEM((n_chip, channels, block), BF16),
            pltpu.VMEM(we_shape, BF16),
            pltpu.VMEM((n_ctx, tokens, 2 * width), BF16),
            pltpu.VMEM((n_ctx, tokens, 2 * width), BF16),
            pltpu.VMEM((nb, 2 * BLOCK, 2 * width), F32),
            pltpu.VMEM((nb, 2 * BLOCK, width), F32),
            pltpu.VMEM((n_ctx, 2 * BLOCK, width), F32),
            pltpu.VMEM((n_ctx // 2, 2 * BLOCK, 2 * width), BF16),
            pltpu.VMEM((n_ctx // 2, 2 * BLOCK, 2 * width), BF16),
            pltpu.VMEM((n_ctx, tokens, width), BF16),
            pltpu.VMEM((n_ctx, tokens, width), BF16),
            pltpu.VMEM((tokens, channels), BF16),
            pltpu.VMEM((tokens, channels), BF16),
        ] + [pltpu.VMEM(shape, BF16) for shape in flows] + [
            pltpu.VMEM((tokens, block), F32),
            pltpu.VMEM((tokens, block) if relay else tiny, F32),
            dma((3, per)), dma((3,)), dma((n_chip,)), dma((n_chip,)), dma((n_chip,)),
            dma((2, 2)), dma((2, 2)), dma((2,)),
            dma((n_ctx, per)), dma((n_ctx, per)), dma((n_ctx, pieces)), dma((n_ctx, pieces)),
            dma((pieces,)), dma((pieces,)),
        ] + [dma(shape) for shape in flow_sems],
        compiler_params=pltpu.CompilerParams(
            collective_id=0, has_side_effects=True, vmem_limit_bytes=VMEM_MIB * 1024 * 1024
        ),
        cost_estimate=pl.CostEstimate(
            flops=28 * n_ctx * tokens * BLOCK * width + 2 * tokens * channels * n_ch * block,
            bytes_accessed=12 * tokens * channels + 2 * channels * n_ch * block, transcendentals=0,
        ),
    )(queries, key_input, value_input, filters, skip_gain[None, :],
      jnp.asarray(forward), jnp.asarray(backward), out_weight)


def solution(mesh):
    in_specs = (
        P("ctx", "ch"),
        P("ctx", "ch"),
        P("ctx", "ch"),
        P("ctx", "ch"),
        P("ch"),
        P("ch", None),
    )
    return jax.shard_map(
        per_device, mesh=mesh, in_specs=in_specs, out_specs=P("ctx", "ch"), check_vma=False
    )
```

```python
import functools

import jax
import jax.numpy as jnp
import numpy as np
from jax import lax
from jax.experimental import pallas as pl
from jax.experimental.pallas import tpu as pltpu
from jax.sharding import PartitionSpec as P

BLOCK = 256
PIECE = 128
SUB = 128
WINDOW = 3
AHEAD = 1
B_LAG = 2
VMEM_MIB = 56
F32 = jnp.float32
BF16 = jnp.bfloat16


def transform_tables(block):
    k = np.arange(block)[:, None]
    n = np.arange(block)[None, :]
    angle = np.pi * (((2 * k + 1) * n) % (4 * block)) / (2 * block)
    forward = np.concatenate([np.cos(angle), -np.sin(angle)], axis=0)
    backward = np.concatenate([np.cos(angle).T, -np.sin(angle).T], axis=1) / block

    def halves(table):
        high = table.astype(BF16)
        low = (table - high.astype(np.float64)).astype(BF16)
        return high, low

    f_high, f_low = halves(forward)
    b_high, b_low = halves(backward)
    return np.stack([f_high, f_low]), np.stack([b_high, b_low])


def dot(left, right):
    return jnp.dot(left, right, preferred_element_type=F32)


MESH = pl.DeviceIdType.MESH


def layer_kernel(n_ctx, n_ch, relay, q_hbm, k_hbm, v_hbm, h_hbm, skip_ref, f_hbm, b_hbm, w_hbm, out_hbm,
                 out_ref, out_sem, q_ref, k_ref, v_ref, h_ref, f_ref, b_ref, w_own, wx, we,
                 outbox, inbox, spec, zbuf, ybuf, yhigh, ylow, conv_out, conv_in, g_ref, gx,
                 send_a, send_b, send_c, recv_a, recv_b, recv_c, ge, gex, own, ahead_c,
                 load_sem, table_sem, w_sem, w_send, w_recv, we_send, we_recv, we_fwd,
                 in_send, in_recv, back_send, back_recv, g_send, g_recv,
                 a_send, a_recv, b_send, b_recv, c_send, c_recv, ge_send, ge_recv, gex_send, gex_recv):
    me = lax.axis_index("ctx")
    ch = lax.axis_index("ch")
    chip = lax.div(ch, 2)
    core = lax.rem(ch, 2)
    mate = ch + 1 - 2 * core
    n_chip = n_ch // 2
    tokens, block = out_ref.shape
    width = conv_in.shape[2]
    per = tokens // BLOCK
    halves = BLOCK // PIECE
    has_left = chip > 0
    has_right = chip < n_chip - 1
    left = jnp.maximum(ch - 2, core)
    right = jnp.minimum(ch + 2, n_ch - 2 + core)

    def remote(src, dst, sent, arrived, target):
        return pltpu.make_async_remote_copy(
            src_ref=src, dst_ref=dst, send_sem=sent, recv_sem=arrived,
            device_id=target, device_id_type=MESH,
        )

    def rows_of(r, size=BLOCK):
        return pl.ds(pl.multiple_of(r * size, size), size)

    barrier = pltpu.get_barrier_semaphore()

    def greet(target):
        pl.semaphore_signal(barrier, inc=1, device_id=target, device_id_type=MESH)

    greet({"ch": mate})
    for d in range(1, n_ctx):
        greet({"ctx": lax.rem(me + d, n_ctx)})

    @pl.when(has_left)
    def _():
        greet({"ch": left})
        greet({"ch": left + 1 - 2 * core})

    @pl.when(has_right)
    def _():
        greet({"ch": right})
        greet({"ch": right + 1 - 2 * core})

    def load(a, r):
        source, target = ((k_hbm, k_ref), (v_hbm, v_ref), (h_hbm, h_ref))[a]
        at = rows_of(r)
        return pltpu.make_async_copy(source.at[at], target.at[at], load_sem.at[a, r])

    f_load = pltpu.make_async_copy(f_hbm, f_ref, table_sem.at[0])
    b_load = pltpu.make_async_copy(b_hbm, b_ref, table_sem.at[1])
    q_load = pltpu.make_async_copy(q_hbm, q_ref, table_sem.at[2])

    def lanes_of(chip_at, core_at):
        return pl.ds(pl.multiple_of((chip_at * 2 + core_at) * block, block), block)

    def w_load(t):
        return pltpu.make_async_copy(w_hbm.at[:, lanes_of(t, core)], w_own.at[t], w_sem.at[t])

    def w_copy(t):
        return remote(w_hbm.at[:, lanes_of(t, 1 - core)], wx.at[t], w_send.at[t], w_recv.at[t], {"ch": mate})

    for r in range(per):
        for a in range(3):
            load(a, r).start()
    f_load.start()

    def in_copy(i, r):
        at = rows_of(r)
        return remote(outbox.at[i, at], inbox.at[me, at], in_send.at[i, r], in_recv.at[me, r], {"ctx": i})

    def in_arrival(i, r):
        at = rows_of(r)
        return remote(outbox.at[i, at], inbox.at[i, at], in_send.at[i, r], in_recv.at[i, r], {"ctx": i})

    pl.semaphore_wait(
        barrier, n_ctx + 2 * has_left.astype(jnp.int32) + 2 * has_right.astype(jnp.int32)
    )

    def fill(r, carry):
        for a in range(3):
            load(a, r).wait()
        at = rows_of(r)
        for i in range(n_ctx):
            lanes = slice(i * width, (i + 1) * width)
            mixed = k_ref[at, lanes].astype(F32) * v_ref[at, lanes].astype(F32)
            outbox[i, at, :width] = mixed.astype(BF16)
            outbox[i, at, width:] = h_ref[at, lanes]

            @pl.when(me != i)
            def _():
                in_copy(i, r).start()
        return carry

    lax.fori_loop(0, per, fill, 0)

    low = 1 - lax.div(chip, n_chip // 2)
    is_end = jnp.logical_or(chip == 0, chip == n_chip - 1)
    is_mid = jnp.logical_not(is_end)
    far = (n_chip - 1) * low
    end = (n_chip - 1) * (1 - low)
    across = n_chip - 1 - chip
    inner = 2 - low

    def bit_of(core_at):
        return (1 - core_at) * lax.rem(me, 2) + core_at * lax.div(me, 2)

    bit = bit_of(core)
    partner = (1 - core) * (me + 1 - 2 * lax.rem(me, 2)) + core * lax.rem(me + 2, 4)

    def we_copy(slot, core_at):
        column = inner * (1 - slot) + (n_chip - 1 - inner) * slot
        return remote(w_hbm.at[:, lanes_of(column, core_at)], we.at[slot, core],
                      we_send.at[slot, core_at], we_recv.at[slot, core], {"ch": inner * 2 + core_at})

    def we_arrival(slot, half):
        return remote(we.at[slot, half], we.at[slot, half], we_fwd.at[slot], we_recv.at[slot, half],
                      {"ctx": partner})

    if relay:
        for core_at in range(2):
            @pl.when(jnp.logical_and(is_end, bit_of(core_at) == core))
            def _():
                for slot in range(2):
                    we_copy(slot, core_at).start()

    b_load.start()
    q_load.start()
    for t in range(n_chip):
        w_load(t).start()
        w_copy(t).start()

    def ahead(box, source, r):
        data = box[source, rows_of(r), :]
        spec[source * per + r] = dot(f_ref[0], data) + dot(f_ref[1], data)

    f_load.wait()

    def ahead_own(r, carry):
        ahead(outbox, me, r)
        return carry

    lax.fori_loop(0, per, ahead_own, 0)

    def ahead_others(r, carry):
        for d in range(1, n_ctx):
            source = lax.rem(me + d, n_ctx)
            in_arrival(source, r).wait_recv()
            ahead(inbox, source, r)
        return carry

    nb = n_ctx * per
    rows = 8
    sign = 1.0 - 2.0 * (lax.broadcasted_iota(jnp.int32, (rows, width), 0) % 2).astype(F32)

    def parts_of(chunk):
        top = pl.multiple_of(chunk * rows, rows)
        return pl.ds(top, rows), pl.ds(pl.multiple_of(BLOCK + top, rows), rows)

    def is_last(p):
        return p % per == per - 1

    def sums(blocks, late, start, re, im):
        pairs = {j: [p for p in range(j + 1) if (is_last(p) or is_last(j - p)) == late] for j in blocks}
        used = {p for j in blocks for p in pairs[j]} | {j - p for j in blocks for p in pairs[j]}
        x = {p: (spec[p, re, :width], spec[p, im, :width]) for p in used}
        h = {p: (spec[p, re, width:], spec[p, im, width:]) for p in used}
        z = {}
        for j in blocks:
            zr, zi = start[j] if j in start else (None, None)
            for p in pairs[j]:
                xr, xi = x[p]
                hr, hi = h[j - p]
                tr = xr * hr - xi * hi
                ti = xr * hi + xi * hr
                zr = tr if zr is None else zr + tr
                zi = ti if zi is None else zi + ti
            z[j] = (zr, zi)
        return z

    def has_early(j):
        return any(not is_last(p) and not is_last(j - p) for p in range(j + 1))

    early = [j for j in range(nb) if has_early(j)]

    def early_sums(chunk, carry):
        re, im = parts_of(chunk)
        for j, (zr, zi) in sums(early, False, {}, re, im).items():
            zbuf[j, re, :] = zr
            zbuf[j, im, :] = zi
        return carry

    lax.fori_loop(0, per - 1, ahead_others, 0)
    lax.fori_loop(0, BLOCK // rows, early_sums, 0)
    ahead_others(per - 1, 0)
    b_load.wait()
    done = set()

    def products(m):
        mine = [i * per + m for i in range(n_ctx)]
        need = sorted(set(mine) | {j - 1 for j in mine if j > 0})
        fresh = [j for j in need if j not in done]
        done.update(fresh)

        def one(chunk, carry):
            re, im = parts_of(chunk)
            start = {j: (zbuf[j, re, :], zbuf[j, im, :]) for j in fresh if j in early}
            z = sums(fresh, True, start, re, im)
            for j in fresh:
                zbuf[j, re, :] = z[j][0]
                zbuf[j, im, :] = z[j][1]

            def get(j):
                return z[j] if j in z else (zbuf[j, re, :], zbuf[j, im, :])

            for i, j in enumerate(mine):
                yr, yi = get(j)
                if j > 0:
                    lr, li = get(j - 1)
                    yr = yr - sign * li
                    yi = yi + sign * lr
                ybuf[i, re, :] = yr
                ybuf[i, im, :] = yi
            return carry

        lax.fori_loop(0, BLOCK // rows, one, 0)
        for i in range(0, n_ctx, 2):
            data = jnp.concatenate([ybuf[i], ybuf[i + 1]], axis=1)
            high = data.astype(BF16)
            yhigh[i // 2] = high
            ylow[i // 2] = (data - high.astype(F32)).astype(BF16)

    def piece(m):
        return rows_of(m, PIECE)

    def back_copy(i, m):
        at = piece(m)
        return remote(conv_out.at[i, at], conv_in.at[me, at], back_send.at[i, m], back_recv.at[me, m], {"ctx": i})

    def back_arrival(i, m):
        at = piece(m)
        return remote(conv_out.at[i, at], conv_in.at[i, at], back_send.at[i, m], back_recv.at[i, m], {"ctx": i})

    def inverse(m):
        at = piece(m)
        inside = slice((m % halves) * PIECE, (m % halves + 1) * PIECE)
        b_high = b_ref[0, inside, :]
        b_low = b_ref[1, inside, :]
        for i in range(0, n_ctx, 2):
            high = yhigh[i // 2]
            conv = (dot(b_high, high) + (dot(b_high, ylow[i // 2]) + dot(b_low, high))).astype(BF16)
            for o in range(2):
                part = conv[:, o * width:(o + 1) * width]
                conv_out[i + o, at, :] = part

                @pl.when(me == i + o)
                def _():
                    conv_in[i + o, at, :] = part

                @pl.when(me != i + o)
                def _():
                    back_copy(i + o, m).start()

    def out_copy(m):
        at = piece(m)
        return pltpu.make_async_copy(out_ref.at[at], out_hbm.at[at], out_sem.at[m])

    def g_copy(m):
        at = piece(m)
        return remote(g_ref.at[at], gx.at[at], g_send.at[m], g_recv.at[m], {"ch": mate})

    def gate(m):
        at = piece(m)
        for i in range(n_ctx):
            @pl.when(me != i)
            def _():
                back_arrival(i, m).wait_recv()

        for i in range(n_ctx):
            lanes = slice(i * width, (i + 1) * width)
            mixed = outbox[i, at, :width].astype(F32)
            total = conv_in[i, at, :].astype(F32) + skip_ref[:, lanes] * mixed
            g_ref[at, lanes] = (q_ref[at, lanes].astype(F32) * total).astype(BF16)
        g_copy(m).start()

    def share(t, at):
        return dot(g_ref[at, :], w_own[t]) + dot(gx[at, :], wx[t])

    def weights_ready():
        for t in range(n_chip):
            w_load(t).wait()
            w_copy(t).wait()

    if relay:
        n_sub = tokens // SUB
        each = PIECE // SUB
        n_piece = tokens // PIECE
        to_inner = {"ch": inner * 2 + core}
        to_end = {"ch": end * 2 + core}
        to_across = {"ch": across * 2 + core}

        def sub(s):
            return rows_of(s, SUB)

        def a_from_end(s):
            return remote(send_a.at[sub(s)], recv_a.at[sub(s)], a_send.at[s], a_recv.at[s], to_inner)

        def a_from_mid(s):
            return remote(send_a.at[sub(s)], recv_b.at[sub(s)], a_send.at[s], b_recv.at[s], to_across)

        def b_from_mid(s):
            return remote(send_b.at[sub(s)], recv_b.at[sub(s)], b_send.at[s], b_recv.at[s], to_end)

        def a_arrival(s):
            return remote(send_a.at[sub(s)], recv_a.at[sub(s)], a_send.at[s], a_recv.at[s], to_end)

        def b_arrival(s):
            return remote(send_b.at[sub(s)], recv_b.at[sub(s)], b_send.at[s], b_recv.at[s], to_across)

        def c_copy(s):
            return remote(send_c.at[sub(s)], recv_c.at[sub(s)], c_send.at[s], c_recv.at[s], to_across)

        def ge_copy(s):
            return remote(g_ref.at[sub(s)], ge.at[sub(s)], ge_send.at[s], ge_recv.at[s], to_inner)

        def ge_arrival(s):
            return remote(g_ref.at[sub(s)], ge.at[sub(s)], ge_send.at[s], ge_recv.at[s], to_end)

        def gex_copy(s):
            return remote(ge.at[sub(s)], gex.at[sub(s)], gex_send.at[s], gex_recv.at[s], {"ch": mate})

        def end_first(m):
            @pl.when(is_end)
            def _():
                g_copy(m).wait()
                part = share(far, piece(m))
                for o in range(each):
                    s = m * each + o
                    send_a[sub(s), :] = part[o * SUB:(o + 1) * SUB].astype(BF16)
                    if s >= WINDOW:
                        a_from_end(s - WINDOW).wait_send()
                    a_from_end(s).start()

        def b_step(s):
            b_arrival(s).wait_recv()
            send_b[sub(s), :] = (own[sub(s), :] + recv_b[sub(s), :].astype(F32)).astype(BF16)
            b_from_mid(s).start()

        def mid_first(m):
            @pl.when(is_mid)
            def _():
                g_copy(m).wait()
                own[piece(m), :] = share(end, piece(m))
                part = share(far, piece(m))
                for o in range(each):
                    s = m * each + o
                    a_arrival(s).wait_recv()
                    send_a[sub(s), :] = (
                        part[o * SUB:(o + 1) * SUB] + recv_a[sub(s), :].astype(F32)
                    ).astype(BF16)
                    a_from_mid(s).start()
                    if s >= B_LAG:
                        b_step(s - B_LAG)

        def pass_weights():
            @pl.when(is_mid)
            def _():
                for slot in range(2):
                    we_arrival(slot, bit).wait_recv()
                    we_arrival(slot, bit).start()

        products(0)
        inverse(0)
        inverse(1)
        products(1)
        q_load.wait()
        gate(0)

        @pl.when(is_end)
        def _():
            for s in range(AHEAD):
                ge_copy(s).start()

        weights_ready()
        inverse(2)
        end_first(0)
        gate(1)
        inverse(3)
        end_first(1)
        products(2)
        gate(2)
        inverse(4)
        end_first(2)
        mid_first(0)
        gate(3)
        inverse(5)
        end_first(3)
        mid_first(1)
        products(3)
        inverse(6)
        inverse(7)
        pass_weights()
        for m in range(4, 8):
            gate(m)
            end_first(m)
            mid_first(m - 2)
        mid_first(6)

        def own_shares(p):
            at = piece(p)
            ahead_c[at, :] = share(across, at)
            own[at, :] = share(chip, at)

        @pl.when(is_mid)
        def _():
            own_shares(0)

        mid_first(7)

        @pl.when(is_end)
        def _():
            for s in range(n_sub - WINDOW, n_sub):
                a_from_end(s).wait_send()

            def step(p, carry):
                for o in range(each):
                    s = p * each + o

                    @pl.when(s >= WINDOW)
                    def _():
                        ge_copy(s - WINDOW).wait_send()

                    @pl.when(s >= AHEAD)
                    def _():
                        ge_copy(s).start()

                at = piece(p)
                part = share(chip, at)
                for o in range(each):
                    b_arrival(p * each + o).wait_recv()
                out_ref[at, :] = (part + recv_b[at, :].astype(F32)).astype(BF16)
                out_copy(p).start()
                return carry

            lax.fori_loop(0, n_piece, step, 0)
            for s in range(n_sub - WINDOW, n_sub):
                ge_copy(s).wait_send()

        @pl.when(is_mid)
        def _():
            for slot in range(2):
                we_arrival(slot, 1 - bit).wait_recv()

            def finish(p):
                at = piece(p)
                for o in range(each):
                    c_copy(p * each + o).wait_recv()
                out_ref[at, :] = (own[at, :] + recv_c[at, :].astype(F32)).astype(BF16)
                out_copy(p).start()

            def relay_rows(at, subs, between):
                for s in subs:
                    ge_arrival(s).wait_recv()
                    gex_copy(s).start()
                part = ahead_c[at, :] + dot(ge[at, :], we[1, core])
                own[at, :] += dot(ge[at, :], we[0, core])
                between()
                for s in subs:
                    gex_copy(s).wait_recv()
                send_c[at, :] = (part + dot(gex[at, :], we[1, 1 - core])).astype(BF16)
                for s in subs:
                    c_copy(s).start()
                own[at, :] += dot(gex[at, :], we[0, 1 - core])

            def relay_piece(p, between):
                relay_rows(piece(p), [p * each + o for o in range(each)], between)

            def nothing():
                pass

            late = list(range(n_sub - B_LAG, n_sub))
            for s in range(each):
                relay_rows(sub(s), [s], (lambda: own_shares(1)) if s == each - 1 else nothing)
                if s > 0:
                    b_step(late.pop(0))
            for p in range(1, 3):
                relay_piece(p, functools.partial(own_shares, p + 1))
                for s in late[:2]:
                    b_step(s)
                late = late[2:]
            for s in late:
                b_step(s)

            def step(p, carry):
                def between():
                    own_shares(p + 1)
                    finish(p - 3)

                relay_piece(p, between)
                return carry

            lax.fori_loop(3, n_piece - 1, step, 0)
            for s in range(n_sub - each, n_sub):
                relay_rows(sub(s), [s], (lambda: finish(n_piece - 4)) if s == n_sub - each else nothing)
            for p in range(n_piece - 3, n_piece):
                finish(p)

            def drain(s, carry):
                a_from_mid(s).wait_send()
                b_from_mid(s).wait_send()
                c_copy(s).wait_send()
                gex_copy(s).wait_send()
                return carry

            lax.fori_loop(0, n_sub, drain, 0)
            for slot in range(2):
                we_arrival(slot, bit).wait_send()

        for core_at in range(2):
            @pl.when(jnp.logical_and(is_end, bit_of(core_at) == core))
            def _():
                for slot in range(2):
                    we_copy(slot, core_at).wait_send()
    else:
        def to_right(t, m):
            at = rows_of(m)
            return remote(send_a.at[t, at], recv_a.at[t, at], a_send.at[t, m], a_recv.at[t, m], {"ch": right})

        def to_left(t, m):
            at = rows_of(m)
            return remote(send_a.at[t, at], recv_b.at[t, at], a_send.at[t, m], b_recv.at[t, m], {"ch": left})

        def arrive_left(t, m):
            at = rows_of(m)
            return remote(send_a.at[t, at], recv_a.at[t, at], a_send.at[t, m], a_recv.at[t, m], {"ch": left})

        def arrive_right(t, m):
            at = rows_of(m)
            return remote(send_a.at[t, at], recv_b.at[t, at], a_send.at[t, m], b_recv.at[t, m], {"ch": right})

        def pass_on(t, m, first, arrived, buffer, copy):
            at = rows_of(m)
            part = share(t, at)

            @pl.when(first)
            def _():
                send_a[t, at, :] = part.astype(BF16)

            @pl.when(jnp.logical_not(first))
            def _():
                arrived(t, m).wait_recv()
                send_a[t, at, :] = (part + buffer[t, at, :].astype(F32)).astype(BF16)

            copy(t, m).start()

        def step(m, carry):
            for o in range(halves):
                g_copy(m * halves + o).wait()
            for d in range(n_chip - 1, 0, -1):
                @pl.when(chip + d < n_chip)
                def _():
                    pass_on(chip + d, m, jnp.logical_not(has_left), arrive_left, recv_a, to_right)

                @pl.when(chip - d >= 0)
                def _():
                    pass_on(chip - d, m, jnp.logical_not(has_right), arrive_right, recv_b, to_left)

            own[rows_of(m), :] = share(chip, rows_of(m))
            return carry

        def finish(m, carry):
            at = rows_of(m)

            @pl.when(has_left)
            def _():
                arrive_left(chip, m).wait_recv()
                own[at, :] += recv_a[chip, at, :].astype(F32)

            @pl.when(has_right)
            def _():
                arrive_right(chip, m).wait_recv()
                own[at, :] += recv_b[chip, at, :].astype(F32)

            out_ref[at, :] = own[at, :].astype(BF16)
            for o in range(halves):
                out_copy(m * halves + o).start()
            for d in range(n_chip - 1, 0, -1):
                @pl.when(chip + d < n_chip)
                def _():
                    to_right(chip + d, m).wait_send()

                @pl.when(chip - d >= 0)
                def _():
                    to_left(chip - d, m).wait_send()
            return carry

        q_load.wait()
        for m in range(per):
            products(m)
            for o in range(halves):
                inverse(m * halves + o)
            if m > 0:
                for o in range(halves):
                    gate((m - 1) * halves + o)
        for o in range(halves):
            gate((per - 1) * halves + o)
        weights_ready()
        lax.fori_loop(0, per, step, 0)
        lax.fori_loop(0, per, finish, 0)

    def drain_ctx(r, carry):
        for i in range(n_ctx):
            @pl.when(me != i)
            def _():
                in_copy(i, r).wait_send()
                for o in range(halves):
                    back_copy(i, r * halves + o).wait_send()
        return carry

    lax.fori_loop(0, per, drain_ctx, 0)

    def drain_out(m, carry):
        out_copy(m).wait()
        return carry

    lax.fori_loop(0, tokens // PIECE, drain_out, 0)


def per_device(queries, key_input, value_input, filters, skip_gain, out_weight):
    tokens, channels = queries.shape
    n_ctx = lax.axis_size("ctx")
    n_ch = lax.axis_size("ch")
    n_chip = n_ch // 2
    block = out_weight.shape[1] // n_ch
    width = channels // n_ctx
    per = tokens // BLOCK
    nb = n_ctx * per
    relay = n_chip == 4 and n_ctx == 4 and per == 4
    forward, backward = transform_tables(BLOCK)
    vmem = pl.BlockSpec(memory_space=pltpu.VMEM)
    hbm = pl.BlockSpec(memory_space=pl.ANY)
    dma = pltpu.SemaphoreType.DMA
    n_sub = tokens // SUB
    pieces = tokens // PIECE
    tiny = (16, 128)
    if relay:
        flows = [(tokens, block)] * 6 + [(tokens, channels)] * 2
        flow_sems = [(n_sub,)] * 10
        we_shape = (2, 2, channels, block)
    else:
        wide = (n_chip, tokens, block)
        flows = [wide, tiny, tiny, wide, wide, tiny, tiny, tiny]
        flow_sems = [(n_chip, per)] * 10
        we_shape = (2, 2, 16, 128)
    return pl.pallas_call(
        functools.partial(layer_kernel, n_ctx, n_ch, relay),
        out_shape=jax.ShapeDtypeStruct((tokens, block), BF16),
        in_specs=[hbm] * 4 + [vmem] + [hbm] * 3,
        out_specs=hbm,
        scratch_shapes=[
            pltpu.VMEM((tokens, block), BF16),
            dma((pieces,)),
            pltpu.VMEM((tokens, channels), BF16),
            pltpu.VMEM((tokens, channels), BF16),
            pltpu.VMEM((tokens, channels), BF16),
            pltpu.VMEM((tokens, channels), BF16),
            pltpu.VMEM(forward.shape, BF16),
            pltpu.VMEM(backward.shape, BF16),
            pltpu.VMEM((n_chip, channels, block), BF16),
            pltpu.VMEM((n_chip, channels, block), BF16),
            pltpu.VMEM(we_shape, BF16),
            pltpu.VMEM((n_ctx, tokens, 2 * width), BF16),
            pltpu.VMEM((n_ctx, tokens, 2 * width), BF16),
            pltpu.VMEM((nb, 2 * BLOCK, 2 * width), F32),
            pltpu.VMEM((nb, 2 * BLOCK, width), F32),
            pltpu.VMEM((n_ctx, 2 * BLOCK, width), F32),
            pltpu.VMEM((n_ctx // 2, 2 * BLOCK, 2 * width), BF16),
            pltpu.VMEM((n_ctx // 2, 2 * BLOCK, 2 * width), BF16),
            pltpu.VMEM((n_ctx, tokens, width), BF16),
            pltpu.VMEM((n_ctx, tokens, width), BF16),
            pltpu.VMEM((tokens, channels), BF16),
            pltpu.VMEM((tokens, channels), BF16),
        ] + [pltpu.VMEM(shape, BF16) for shape in flows] + [
            pltpu.VMEM((tokens, block), F32),
            pltpu.VMEM((tokens, block) if relay else tiny, F32),
            dma((3, per)), dma((3,)), dma((n_chip,)), dma((n_chip,)), dma((n_chip,)),
            dma((2, 2)), dma((2, 2)), dma((2,)),
            dma((n_ctx, per)), dma((n_ctx, per)), dma((n_ctx, pieces)), dma((n_ctx, pieces)),
            dma((pieces,)), dma((pieces,)),
        ] + [dma(shape) for shape in flow_sems],
        compiler_params=pltpu.CompilerParams(
            collective_id=0, has_side_effects=True, vmem_limit_bytes=VMEM_MIB * 1024 * 1024
        ),
        cost_estimate=pl.CostEstimate(
            flops=28 * n_ctx * tokens * BLOCK * width + 2 * tokens * channels * n_ch * block,
            bytes_accessed=12 * tokens * channels + 2 * channels * n_ch * block, transcendentals=0,
        ),
    )(queries, key_input, value_input, filters, skip_gain[None, :],
      jnp.asarray(forward), jnp.asarray(backward), out_weight)


def solution(mesh):
    in_specs = (
        P("ctx", "ch"),
        P("ctx", "ch"),
        P("ctx", "ch"),
        P("ctx", "ch"),
        P("ch"),
        P("ch", None),
    )
    return jax.shard_map(
        per_device, mesh=mesh, in_specs=in_specs, out_specs=P("ctx", "ch"), check_vma=False
    )
```
